256 devices in a mesh: dom: 128 (over x, z, y), feat: 2 (over core).
Axes of the slice: x: 4, y: 4, z: 8, core: 2. Of those that a mesh axis runs over, the one named last changes fastest.
Arguments:
- node_lat: bfloat16 [131072, 512], P('dom'), may hold values from -6 to 6
- edge_lat: bfloat16 [262144, 512], P(('dom', 'feat')), may hold values from -6 to 6
- edge_src: int32 [262144], P(('dom', 'feat')), may hold values from 0 to 1535
- edge_dst: int32 [262144], P(('dom', 'feat')), may hold values from 0 to 1023
- halo_rows: int32 [1024, 64], P('dom'), may hold values from 0 to 1023
- probe_rows: int32 [2048, 128], P(('dom', 'feat')), may hold values from 0 to 1023
- probe_slot: int32 [131072, 8], P(('dom', 'feat')), may hold values from 0 to 1023
- probe_wgt: float32 [131072, 8], P(('dom', 'feat')), may hold values from 0.05 to 0.3
- probe_embed: bfloat16 [131072, 512], P(('dom', 'feat')), may hold values from -6 to 6
- edge_first: bfloat16 [2, 1536, 512], replicated, may hold values from -0.15625 to 0.15625
- edge_second: bfloat16 [2, 512, 512], replicated, may hold values from -0.25 to 0.25
- node_first: bfloat16 [2, 1024, 512], replicated, may hold values from -0.1875 to 0.1875
- node_second: bfloat16 [2, 512, 512], replicated, may hold values from -0.25 to 0.25
- decode_first: bfloat16 [512, 512], replicated, may hold values from -0.25 to 0.25
- decode_second: bfloat16 [4, 512], replicated, may hold values from -0.25 to 0.25
Outputs:
- surface_out: bfloat16 [131072, 512], P('dom')
- fields: float32 [4, 131072], P(None, ('dom', 'feat'))
The draws below stay inside these ranges and needn't reach their ends.
All inputs are finite; a program needn't handle non-finite values.
Results may differ from the reference program's by a relative error of at most 0.013.
Values may be sent and summed in bfloat16 or wider, within the bound.
A program may use at most 64 MiB of HBM per device.

```python
import math
import jax
import jax.numpy as jnp
import numpy as np
from jax import lax

D = 512
LAYERS = 2
NBR = 8
OUTC = 4
NEIGH = 8
SPAN = 4
NODE_DEV = 1024
EDGE_DEV = 1024
HALO_DEV = 512
REQ_DEV = 1024
PROBE_DEV = 512
HSLOT = 64
QSLOT = 128
EXT = 1536
NODES = 131072
EDGES = 262144
PROBES = 131072
N_DOM = 128
N_FEAT = 2


def touch_ends(entries, rng, smallest, largest):
    spot = [jax.random.randint(jax.random.fold_in(rng, axis), (), 0, length) for axis, length in enumerate(entries.shape)]
    longest = entries.shape.index(max(entries.shape))
    beside = spot[:longest] + [(spot[longest] + 1) % entries.shape[longest]] + spot[longest + 1:]
    return entries.at[tuple(spot)].set(smallest).at[tuple(beside)].set(largest)


def block_levels(key, extent, pieces, low, high):
    def one(position, parts):
        heights = jax.random.uniform(jax.random.fold_in(jax.random.fold_in(key, 6), position), (parts,), jnp.float32, low / len(pieces), high / len(pieces))
        return jnp.repeat(jnp.exp(heights), extent[position] // parts).reshape((-1,) + (1,) * (len(extent) - position - 1))

    level = one(*pieces[0])
    for cut in pieces[1:]:
        level = level * one(*cut)
    return level


def cumulative_ranks(amount, lean):
    weights = [(1 << 20) // math.isqrt(standing ** lean) + 1 for standing in range(1, amount + 1)]
    scale = 1 + sum(weights) // (1 << 30)
    return np.cumsum(np.array([max(1, weight // scale) for weight in weights]))


def ranked_ids(key, dims, count, lean):
    listing = cumulative_ranks(count, lean)
    ticket = jax.random.randint(jax.random.fold_in(key, 1), dims, 0, int(listing[count - 1]))
    rank = jnp.searchsorted(jnp.asarray(listing, jnp.int32), ticket, side="right")
    return jax.random.permutation(jax.random.fold_in(key, 2), count)[rank].astype(jnp.int32)


def bell_draw(rng, extent, deviation, most, shards=(), held_as=jnp.bfloat16):
    loudness = block_levels(rng, extent, shards, -0.22, 0.18) if shards else 1.0
    drawn = jax.random.normal(rng, extent, jnp.float32) * deviation * loudness
    return jnp.minimum(jnp.maximum(drawn, -most), most).astype(held_as)


def setup_inputs(seed: int = 0) -> dict:
    seeds = jax.random.split(jax.random.key(seed), 16)
    return {
        "node_lat": bell_draw(seeds[0], (NODES, D), 1.0, 6.0, ((0, 128),)),
        "edge_lat": bell_draw(seeds[1], (EDGES, D), 1.0, 6.0, ((0, 256),)),
        "edge_src": touch_ends(jax.random.randint(seeds[2], (EDGES,), 0, EXT), jax.random.fold_in(seeds[2], 1), 0, EXT - 1).astype(jnp.int32),
        "edge_dst": touch_ends(jax.random.randint(seeds[3], (EDGES,), 0, NODE_DEV), jax.random.fold_in(seeds[3], 1), 0, NODE_DEV - 1).astype(jnp.int32),
        "halo_rows": touch_ends(jax.random.randint(seeds[4], (N_DOM * NEIGH, HSLOT), 0, NODE_DEV), jax.random.fold_in(seeds[4], 1), 0, NODE_DEV - 1).astype(jnp.int32),
        "probe_rows": touch_ends(jax.random.randint(seeds[5], (N_DOM * N_FEAT * NEIGH, QSLOT), 0, NODE_DEV), jax.random.fold_in(seeds[5], 1), 0, NODE_DEV - 1).astype(jnp.int32),
        "probe_slot": touch_ends(ranked_ids(seeds[6], (PROBES, NBR), REQ_DEV, 2), jax.random.fold_in(seeds[6], 3), 0, REQ_DEV - 1).astype(jnp.int32),
        "probe_wgt": jnp.clip(0.05 + 0.25 * jax.random.uniform(seeds[7], (PROBES, NBR), jnp.float32) ** block_levels(seeds[7], (PROBES, NBR), ((0, 256),), -0.2, 0.2), 0.05, 0.3),
        "probe_embed": bell_draw(seeds[8], (PROBES, D), 1.0, 6.0, ((0, 256),)),
        "edge_first": bell_draw(seeds[9], (LAYERS, 3 * D, D), (3 * D) ** -0.5, 0.15625),
        "edge_second": bell_draw(seeds[10], (LAYERS, D, D), D ** -0.5, 0.25),
        "node_first": bell_draw(seeds[11], (LAYERS, 2 * D, D), (2 * D) ** -0.5, 0.1875),
        "node_second": bell_draw(seeds[12], (LAYERS, D, D), D ** -0.5, 0.25),
        "decode_first": bell_draw(seeds[13], (D, D), D ** -0.5, 0.25),
        "decode_second": bell_draw(seeds[14], (OUTC, D), D ** -0.5, 0.25),
    }


def layer_norm(values):
    centre = lax.optimization_barrier(jnp.mean(values, axis=-1, keepdims=True))
    shifted = values - centre
    spread = lax.optimization_barrier(jnp.mean(shifted * shifted, axis=-1, keepdims=True))
    return shifted * lax.rsqrt(spread + 1e-05)

def neighbour_offsets(width):
    return [1, -1, width, -width, width + 1, -width - 1, width - 1, 1 - width]

def one_layer(node_lat, edge_lat, edge_src, edge_dst, halo_rows, first_e, second_e, first_n, second_n):
    node_blocks = node_lat.reshape(N_DOM, NODE_DEV, D)
    send_rows = halo_rows.reshape(N_DOM, NEIGH, HSLOT)
    sent = jax.vmap(lambda source, picks: jnp.take(source, picks.reshape(-1), axis=0).reshape(NEIGH, HSLOT, D))(node_blocks, send_rows)
    offsets = neighbour_offsets(SPAN)
    halo = jnp.stack([jnp.roll(sent[:, k], offsets[k], axis=0) for k in range(NEIGH)], axis=1)
    halo = halo.reshape(N_DOM, HALO_DEV, D)
    edge_blocks = edge_lat.reshape(N_DOM, N_FEAT * EDGE_DEV, D)
    src_blocks = edge_src.reshape(N_DOM, N_FEAT * EDGE_DEV)
    dst_blocks = edge_dst.reshape(N_DOM, N_FEAT * EDGE_DEV)

    def domain(items):
        own, far, latent, senders, receivers = items
        lookup = jnp.concatenate([own, far], axis=0)
        joined = jnp.concatenate([latent, jnp.take(lookup, senders, axis=0), jnp.take(own, receivers, axis=0)], axis=1)
        hidden = jax.nn.relu(jnp.dot(joined, first_e, preferred_element_type=jnp.float32)).astype(jnp.bfloat16)
        update = jnp.dot(hidden, second_e, preferred_element_type=jnp.float32)
        new_latent = (latent.astype(jnp.float32) + layer_norm(update)).astype(jnp.bfloat16)
        summed = jax.ops.segment_sum(new_latent.astype(jnp.float32), receivers, num_segments=NODE_DEV).astype(jnp.bfloat16)
        joined_nodes = jnp.concatenate([own, summed], axis=1)
        hidden_nodes = jax.nn.relu(jnp.dot(joined_nodes, first_n, preferred_element_type=jnp.float32)).astype(jnp.bfloat16)
        update_nodes = jnp.dot(hidden_nodes, second_n, preferred_element_type=jnp.float32)
        new_own = (own.astype(jnp.float32) + layer_norm(update_nodes)).astype(jnp.bfloat16)
        return (new_own, new_latent)
    new_nodes, new_edges = lax.map(domain, (node_blocks, halo, edge_blocks, src_blocks, dst_blocks))
    return (new_nodes.reshape(NODES, D), new_edges.reshape(EDGES, D))

def reference(node_lat, edge_lat, edge_src, edge_dst, halo_rows, probe_rows, probe_slot, probe_wgt, probe_embed, edge_first, edge_second, node_first, node_second, decode_first, decode_second):
    current_nodes = node_lat
    current_edges = edge_lat
    for section_index in range(LAYERS):
        current_nodes, current_edges = one_layer(current_nodes, current_edges, edge_src, edge_dst, halo_rows, edge_first[section_index], edge_second[section_index], node_first[section_index], node_second[section_index])
    surface_out = current_nodes
    starts = (jnp.arange(N_DOM, dtype=jnp.int32) * NODE_DEV).astype(jnp.int32)
    based = probe_rows.reshape(N_DOM, N_FEAT, NEIGH, QSLOT) + starts[:, None, None, None]
    offsets = neighbour_offsets(SPAN)
    row_ids = jnp.stack([jnp.roll(based[:, :, k], offsets[k], axis=0) for k in range(NEIGH)], axis=2)
    row_ids = row_ids.reshape(N_DOM * N_FEAT, REQ_DEV).astype(jnp.int32)
    slot_blocks = probe_slot.reshape(N_DOM * N_FEAT, PROBE_DEV, NBR)
    global_ids = jax.vmap(lambda table_ids, picks: jnp.take(table_ids, picks, axis=0))(row_ids, slot_blocks)
    global_ids = global_ids.reshape(PROBES, NBR)
    interp = jnp.zeros((PROBES, D), jnp.float32)
    for slot_index in range(NBR):
        picked = jnp.take(surface_out, global_ids[:, slot_index], axis=0).astype(jnp.float32)
        interp = interp + probe_wgt[:, slot_index:slot_index + 1] * picked
    decoder_in = (interp + probe_embed.astype(jnp.float32)).astype(jnp.bfloat16)
    hidden_dec = jax.nn.relu(jnp.dot(decoder_in, decode_first, preferred_element_type=jnp.float32)).astype(jnp.bfloat16)
    fields = lax.dot_general(decode_second, hidden_dec, (((1,), (1,)), ((), ())), preferred_element_type=jnp.float32)
    return (surface_out, fields)
```

```python
import functools

import jax
import jax.numpy as jnp
from jax import lax
from jax.experimental import pallas as pl
from jax.experimental.pallas import tpu as pltpu
from jax.sharding import PartitionSpec as P

SPAN = 4
BF = jnp.bfloat16
F32 = jnp.float32
MESH = pl.DeviceIdType.MESH
OFFSETS = (1, -1, SPAN, -SPAN, SPAN + 1, -SPAN - 1, SPAN - 1, 1 - SPAN)
ROWS = 256


def dot(a, b):
    return jnp.dot(a, b, preferred_element_type=F32)


def layer_norm(values):
    centre = jnp.mean(values, axis=-1, keepdims=True)
    shifted = values - centre
    spread = jnp.mean(shifted * shifted, axis=-1, keepdims=True)
    return shifted * lax.rsqrt(spread + 1e-05)


def tiles(count, body):
    def step(i, carry):
        body(pl.multiple_of(i * ROWS, ROWS))
        return carry

    lax.fori_loop(0, count // ROWS, step, 0)


def column(row):
    return jnp.transpose(jnp.broadcast_to(row, (128, 128)))


def kernel(
    node_hbm, edge_hbm, esrc, edst, hrows, prows, pslot, pwgt, emb_hbm,
    ef_hbm, es_hbm, nf_hbm, ns_hbm, d1_hbm, d2,
    out_hbm, fields,
    h0, h1, h2, edge, emb, ef, es, nf, ns, d1,
    csrc, cdst, chalo, cprobe, ssrc, sdst, tdst, shalo, sprobe, wint,
    own, pre, hn, part, part_in, halo_out, halo_in, probe_out, probe_in,
    load_sem, store_sem, hs_sem, hr_sem, xs_sem, xr_sem, ps_sem, pr_sem,
):
    nodes, edges = h0.shape[0], edge.shape[0]
    halos, requests, probes = halo_in.shape[1], probe_in.shape[0], emb.shape[0]
    hslot, qslot = halos // 8, requests // 8
    count = lax.axis_size("dom")
    dom, feat = lax.axis_index("dom"), lax.axis_index("feat")
    peer = 1 - feat
    targets = [lax.rem(dom + off + count, count) for off in OFFSETS]

    pairs = [
        (node_hbm, h0), (edge_hbm, edge),
        (ef_hbm.at[0], ef.at[0]), (nf_hbm.at[0], nf.at[0]), (es_hbm.at[0], es.at[0]), (ns_hbm.at[0], ns.at[0]),
        (ef_hbm.at[1], ef.at[1]), (nf_hbm.at[1], nf.at[1]), (es_hbm.at[1], es.at[1]), (ns_hbm.at[1], ns.at[1]),
        (emb_hbm, emb), (d1_hbm, d1),
    ]
    loads = [pltpu.make_async_copy(src, dst, load_sem.at[i]) for i, (src, dst) in enumerate(pairs)]
    for load in loads:
        load.start()

    barrier = pltpu.get_barrier_semaphore()
    for target in targets:
        pl.semaphore_signal(barrier, inc=1, device_id=(target, feat), device_id_type=MESH)
    pl.semaphore_signal(barrier, inc=1, device_id=(dom, peer), device_id_type=MESH)

    for j in range(edges // 128):
        csrc[j * 128 : (j + 1) * 128, :] = column(esrc[j : j + 1, :])
        cdst[j * 128 : (j + 1) * 128, :] = column(edst[j : j + 1, :])
    for j in range(requests // 128):
        cprobe[j * 128 : (j + 1) * 128, :] = column(prows[j : j + 1, :])
    for j in range(halos // 128):
        pair = jnp.concatenate([hrows[2 * j : 2 * j + 1, :], hrows[2 * j + 1 : 2 * j + 2, :]], axis=1)
        chalo[j * 128 : (j + 1) * 128, :] = column(pair)

    lanes = lax.broadcasted_iota(jnp.int32, (ROWS, 128), 1)
    sublanes = lax.broadcasted_iota(jnp.int32, (ROWS, 128), 0)

    def select(out, col, r):
        here = col[pl.ds(r, ROWS), :]
        for j in range(out.shape[1] // 128):
            hit = jnp.where(here == lanes + j * 128, 1.0, 0.0).astype(BF)
            out[pl.ds(r, ROWS), j * 128 : (j + 1) * 128] = hit

    tiles(halos, lambda r: select(shalo, chalo, r))
    loads[0].wait()

    def gather_halo(layer, h):
        def go(r):
            halo_out[layer, pl.ds(r, ROWS), :] = dot(shalo[pl.ds(r, ROWS), :], h[...]).astype(BF)

        tiles(halos, go)

    gather_halo(0, h0)

    def halo_copy(layer, k):
        part_k = pl.ds(k * hslot, hslot)
        return pltpu.make_async_remote_copy(
            src_ref=halo_out.at[layer, part_k, :], dst_ref=halo_in.at[layer, part_k, :],
            send_sem=hs_sem.at[layer, k], recv_sem=hr_sem.at[layer, k],
            device_id=(targets[k], feat), device_id_type=MESH,
        )

    def exchange(layer, c):
        rows = pl.ds(c * ROWS, ROWS)
        return pltpu.make_async_remote_copy(
            src_ref=part.at[layer, rows, :], dst_ref=part_in.at[layer, rows, :],
            send_sem=xs_sem.at[layer, c], recv_sem=xr_sem.at[layer, c],
            device_id=(dom, peer), device_id_type=MESH,
        )

    def probe_copy(k):
        part_k = pl.ds(k * qslot, qslot)
        return pltpu.make_async_remote_copy(
            src_ref=probe_out.at[part_k, :], dst_ref=probe_in.at[part_k, :],
            send_sem=ps_sem.at[k], recv_sem=pr_sem.at[k],
            device_id=(targets[k], feat), device_id_type=MESH,
        )

    pl.semaphore_wait(barrier, 9)
    for k in range(8):
        halo_copy(0, k).start()

    def edge_selectors(r):
        select(ssrc, csrc, r)
        select(sdst, cdst, r)

    tiles(edges, edge_selectors)

    def node_selectors(r):
        here = sublanes + r
        for j in range(edges // 128):
            hit = jnp.where(here == edst[j : j + 1, :], 1.0, 0.0).astype(BF)
            tdst[pl.ds(r, ROWS), j * 128 : (j + 1) * 128] = hit

    tiles(nodes, node_selectors)

    def interp_weights(r):
        here = sublanes + r
        for j in range(probes // 128):
            lane = slice(j * 128, (j + 1) * 128)
            total = jnp.zeros((ROWS, 128), F32)
            for s in range(8):
                total = total + jnp.where(here == pslot[s : s + 1, lane], pwgt[s : s + 1, lane], 0.0)
            wint[j * 128 : (j + 1) * 128, pl.ds(r, ROWS)] = jnp.transpose(total).astype(BF)

    def edge_lat_part(layer):
        def go(r):
            rows = pl.ds(r, ROWS)
            pre[rows, :] = dot(edge[rows, :], ef[layer, 0:512, :])

        tiles(edges, go)

    def own_part(layer, h):
        def go(r):
            rows = pl.ds(r, ROWS)
            own[rows, :] = dot(ssrc[rows, 0:nodes], h[...]).astype(BF)
            there = dot(sdst[rows, :], h[...]).astype(BF)
            pre[rows, :] += dot(there, ef[layer, 1024:1536, :])

        tiles(edges, go)

    def edge_update(layer):
        def go(r):
            rows = pl.ds(r, ROWS)
            far = dot(ssrc[rows, nodes:], halo_in[layer]).astype(BF)
            hidden = pre[rows, :] + dot(own[rows, :] + far, ef[layer, 512:1024, :])
            hidden = jnp.maximum(hidden, 0.0).astype(BF)
            update = dot(hidden, es[layer])
            edge[rows, :] = (edge[rows, :].astype(F32) + layer_norm(update)).astype(BF)

        tiles(edges, go)

    def node_lat_part(layer, h):
        def go(r):
            rows = pl.ds(r, ROWS)
            hn[rows, :] = dot(h[rows, :], nf[layer, 0:512, :])

        tiles(nodes, go)

    def sum_edges(layer):
        for c in range(nodes // ROWS):
            rows = slice(c * ROWS, (c + 1) * ROWS)
            part[layer, rows, :] = dot(tdst[rows, :], edge[...]).astype(BF)
            exchange(layer, c).start()

    def node_update(layer, h, new):
        for c in range(nodes // ROWS):
            exchange(layer, c).wait()

        def go(r):
            rows = pl.ds(r, ROWS)
            summed = (part[layer, rows, :].astype(F32) + part_in[layer, rows, :].astype(F32)).astype(BF)
            hidden = hn[rows, :] + dot(summed, nf[layer, 512:1024, :])
            hidden = jnp.maximum(hidden, 0.0).astype(BF)
            update = dot(hidden, ns[layer])
            new[rows, :] = (h[rows, :].astype(F32) + layer_norm(update)).astype(BF)

        tiles(nodes, go)

    loads[1].wait()
    loads[2].wait()
    edge_lat_part(0)
    own_part(0, h0)
    loads[3].wait()
    node_lat_part(0, h0)
    loads[4].wait()
    for k in range(8):
        halo_copy(0, k).wait()
    edge_update(0)
    sum_edges(0)
    loads[6].wait()
    edge_lat_part(1)
    loads[5].wait()
    node_update(0, h0, h1)

    gather_halo(1, h1)
    for k in range(8):
        halo_copy(1, k).start()
    own_part(1, h1)
    loads[7].wait()
    node_lat_part(1, h1)
    loads[8].wait()
    for k in range(8):
        halo_copy(1, k).wait()
    edge_update(1)
    sum_edges(1)
    tiles(requests, lambda r: select(sprobe, cprobe, r))
    loads[9].wait()
    node_update(1, h1, h2)

    store = pltpu.make_async_copy(h2, out_hbm, store_sem.at[0])
    store.start()
    for c in range(4):
        rows = slice(c * 256, (c + 1) * 256)
        probe_out[rows, :] = dot(sprobe[rows, :], h2[...]).astype(BF)
        probe_copy(2 * c).start()
        probe_copy(2 * c + 1).start()
    tiles(requests, interp_weights)
    loads[10].wait()
    loads[11].wait()
    for k in range(8):
        probe_copy(k).wait()

    def decode(r):
        rows = pl.ds(r, ROWS)
        inside = (dot(wint[rows, :], probe_in[...]) + emb[rows, :].astype(F32)).astype(BF)
        hidden = jnp.maximum(dot(inside, d1[...]), 0.0).astype(BF)
        fields[:, pl.ds(r, ROWS)] = lax.dot_general(
            d2[...], hidden, (((1,), (1,)), ((), ())), preferred_element_type=F32
        )

    tiles(probes, decode)
    store.wait()


def body(
    node_lat, edge_lat, edge_src, edge_dst, halo_rows, probe_rows, probe_slot, probe_wgt, probe_embed,
    edge_first, edge_second, node_first, node_second, decode_first, decode_second,
):
    nodes, width = node_lat.shape
    edges, probes = edge_lat.shape[0], probe_embed.shape[0]
    halos, requests = halo_rows.size, probe_rows.size
    layers, fields = edge_first.shape[0], decode_second.shape[0]
    anywhere = pl.BlockSpec(memory_space=pl.ANY)
    vmem = pl.BlockSpec(memory_space=pltpu.VMEM)
    dma = pltpu.SemaphoreType.DMA
    return pl.pallas_call(
        kernel,
        out_shape=(
            jax.ShapeDtypeStruct((nodes, width), BF),
            jax.ShapeDtypeStruct((fields, probes), F32),
        ),
        in_specs=[anywhere] * 2 + [vmem] * 6 + [anywhere] * 6 + [vmem],
        out_specs=(anywhere, vmem),
        scratch_shapes=[
            pltpu.VMEM((nodes, width), BF), pltpu.VMEM((nodes, width), BF), pltpu.VMEM((nodes, width), BF),
            pltpu.VMEM((edges, width), BF), pltpu.VMEM((probes, width), BF),
            pltpu.VMEM(edge_first.shape, BF), pltpu.VMEM(edge_second.shape, BF),
            pltpu.VMEM(node_first.shape, BF), pltpu.VMEM(node_second.shape, BF), pltpu.VMEM(decode_first.shape, BF),
            pltpu.VMEM((edges, 128), jnp.int32), pltpu.VMEM((edges, 128), jnp.int32),
            pltpu.VMEM((halos, 128), jnp.int32), pltpu.VMEM((requests, 128), jnp.int32),
            pltpu.VMEM((edges, nodes + halos), BF), pltpu.VMEM((edges, nodes), BF), pltpu.VMEM((nodes, edges), BF),
            pltpu.VMEM((halos, nodes), BF), pltpu.VMEM((requests, nodes), BF), pltpu.VMEM((probes, requests), BF),
            pltpu.VMEM((edges, width), BF), pltpu.VMEM((edges, width), F32), pltpu.VMEM((nodes, width), F32),
            pltpu.VMEM((layers, nodes, width), BF), pltpu.VMEM((layers, nodes, width), BF),
            pltpu.VMEM((layers, halos, width), BF), pltpu.VMEM((layers, halos, width), BF),
            pltpu.VMEM((requests, width), BF), pltpu.VMEM((requests, width), BF),
            dma((12,)), dma((1,)), dma((layers, 8)), dma((layers, 8)), dma((layers, 4)), dma((layers, 4)),
            dma((8,)), dma((8,)),
        ],
        compiler_params=pltpu.CompilerParams(
            collective_id=0, has_side_effects=True, vmem_limit_bytes=56 * 1024 * 1024
        ),
    )(
        node_lat, edge_lat, edge_src.reshape(-1, 128), edge_dst.reshape(-1, 128), halo_rows, probe_rows,
        probe_slot.T, probe_wgt.T, probe_embed,
        edge_first, edge_second, node_first, node_second, decode_first, decode_second,
    )


def solution(mesh):
    both = P(("dom", "feat"), None)
    return jax.shard_map(
        body,
        mesh=mesh,
        in_specs=(
            P("dom", None), both, P(("dom", "feat")), P(("dom", "feat")), P("dom", None),
            both, both, both, both, P(), P(), P(), P(), P(), P(),
        ),
        out_specs=(P("dom", None), P(None, ("dom", "feat"))),
        check_vma=False,
    )
```

```python
import jax
import jax.numpy as jnp
from jax import lax
from jax.experimental import pallas as pl
from jax.experimental.pallas import tpu as pltpu
from jax.sharding import PartitionSpec as P

SPAN = 4
BF = jnp.bfloat16
F32 = jnp.float32
MESH = pl.DeviceIdType.MESH
OFFSETS = (1, -1, SPAN, -SPAN, SPAN + 1, -SPAN - 1, SPAN - 1, 1 - SPAN)
ROWS = 512
SEL = 256
FAR_FIRST = (2, 3, 0, 1)


def dot(a, b):
    return jnp.dot(a, b, preferred_element_type=F32)


def layer_norm(values):
    centre = jnp.mean(values, axis=-1, keepdims=True)
    shifted = values - centre
    spread = jnp.mean(shifted * shifted, axis=-1, keepdims=True)
    return shifted * lax.rsqrt(spread + 1e-05)


def looped(count, body):
    def step(i, carry):
        body(pl.multiple_of(i * SEL, SEL))
        return carry

    lax.fori_loop(0, count // SEL, step, 0)


def unrolled(count, body):
    for r in range(0, count, ROWS):
        body(slice(r, r + ROWS))


def column(row):
    return jnp.transpose(jnp.broadcast_to(row, (128, 128)))


def kernel(
    node_hbm, edge_hbm, esrc, edst, hrows, prows, pslot, pwgt, emb_hbm,
    ef_hbm, es_hbm, nf_hbm, ns_hbm, d1_hbm, d2,
    out_hbm, fields,
    h0, h1, h2, edge, emb, ef, es, nf, ns, d1,
    csrc, cdst, chalo, cprobe, prows_in, ssrc, sdst, tdst, shalo, thalo, sprobe, tprobe, wint,
    own, pre, hn, hnh, hnp, part, part_in, halo_part, halo_part_in, halo_out, halo_in,
    pick, mine, theirs, theirs_in, probe_out, probe_in,
    load_sem, store_sem, hs_sem, hr_sem, xs_sem, xr_sem, ys_sem, yr_sem, zs_sem, zr_sem, ps_sem, pr_sem, is_sem, ir_sem,
):
    nodes, edges = h0.shape[0], edge.shape[0]
    halos, requests, probes = halo_in.shape[1], probe_in.shape[0], emb.shape[0]
    hslot, qslot = halos // 8, requests // 8
    count = lax.axis_size("dom")
    dom, feat = lax.axis_index("dom"), lax.axis_index("feat")
    peer = 1 - feat
    targets = [lax.rem(dom + off + count, count) for off in OFFSETS]

    barrier = pltpu.get_barrier_semaphore()
    for target in targets:
        pl.semaphore_signal(barrier, inc=1, device_id=(target, feat), device_id_type=MESH)
    pl.semaphore_signal(barrier, inc=1, device_id=(dom, peer), device_id_type=MESH)

    pairs = [
        (node_hbm, h0), (edge_hbm, edge),
        (ef_hbm.at[0], ef.at[0]), (nf_hbm.at[0], nf.at[0]), (es_hbm.at[0], es.at[0]), (ns_hbm.at[0], ns.at[0]),
        (ef_hbm.at[1], ef.at[1]), (nf_hbm.at[1], nf.at[1]), (es_hbm.at[1], es.at[1]), (ns_hbm.at[1], ns.at[1]),
        (emb_hbm, emb), (d1_hbm, d1),
    ]
    loads = [pltpu.make_async_copy(src, dst, load_sem.at[i]) for i, (src, dst) in enumerate(pairs)]
    for load in loads:
        load.start()

    def remote(src, dst, send, recv, device):
        return pltpu.make_async_remote_copy(
            src_ref=src, dst_ref=dst, send_sem=send, recv_sem=recv, device_id=device, device_id_type=MESH
        )

    def halo_copy(layer, k):
        rows = pl.ds(k * hslot, hslot)
        return remote(halo_out.at[layer, rows, :], halo_in.at[layer, rows, :],
                      hs_sem.at[layer, k], hr_sem.at[layer, k], (targets[k], feat))

    def exchange(layer, c):
        rows = pl.ds(c * ROWS, ROWS)
        return remote(part.at[layer, rows, :], part_in.at[layer, rows, :],
                      xs_sem.at[layer, c], xr_sem.at[layer, c], (dom, peer))

    def halo_exchange(c):
        rows = pl.ds(c * SEL, SEL)
        return remote(halo_part.at[rows, :], halo_part_in.at[rows, :], ys_sem.at[c], yr_sem.at[c], (dom, peer))

    def probe_exchange(c):
        rows = pl.ds(c * 2 * qslot, 2 * qslot)
        return remote(theirs.at[rows, :], theirs_in.at[rows, :], zs_sem.at[c], zr_sem.at[c], (dom, peer))

    def probe_copy(k):
        rows = pl.ds(k * qslot, qslot)
        return remote(probe_out.at[rows, :], probe_in.at[rows, :], ps_sem.at[k], pr_sem.at[k], (targets[k], feat))

    index_copy = remote(prows, prows_in, is_sem.at[0], ir_sem.at[0], (dom, peer))

    lanes = lax.broadcasted_iota(jnp.int32, (SEL, 128), 1)
    sublanes = lax.broadcasted_iota(jnp.int32, (SEL, 128), 0)

    def select(out, col, r):
        here = col[pl.ds(r, SEL), :]
        for j in range(out.shape[1] // 128):
            hit = jnp.where(here == lanes + j * 128, 1.0, 0.0).astype(BF)
            out[pl.ds(r, SEL), j * 128 : (j + 1) * 128] = hit

    def incident(out, here, r):
        for j in range(edges // 128):
            hit = jnp.where(here == edst[j : j + 1, :], 1.0, 0.0).astype(BF)
            out[pl.ds(r, SEL), j * 128 : (j + 1) * 128] = hit

    for j in range(halos // 128):
        pair = jnp.concatenate([hrows[2 * j : 2 * j + 1, :], hrows[2 * j + 1 : 2 * j + 2, :]], axis=1)
        chalo[j * 128 : (j + 1) * 128, :] = column(pair)
    looped(halos, lambda r: select(shalo, chalo, r))
    loads[0].wait()
    halo_out[0] = dot(shalo[...], h0[...]).astype(BF)
    pl.semaphore_wait(barrier, 9)
    for k in range(7, -1, -1):
        halo_copy(0, k).start()
    index_copy.start()

    for j in range(edges // 128):
        csrc[j * 128 : (j + 1) * 128, :] = column(esrc[j : j + 1, :])
        cdst[j * 128 : (j + 1) * 128, :] = column(edst[j : j + 1, :])
    looped(edges, lambda r: (select(ssrc, csrc, r), select(sdst, cdst, r), None)[2])

    def edge_lat_part(layer):
        def go(rows):
            pre[rows, :] = dot(edge[rows, :], ef[layer, 0:512, :])

        unrolled(edges, go)

    def own_part(layer, h):
        def go(rows):
            own[rows, :] = dot(ssrc[rows, 0:nodes], h[...]).astype(BF)
            there = dot(sdst[rows, :], h[...]).astype(BF)
            pre[rows, :] += dot(there, ef[layer, 1024:1536, :])

        unrolled(edges, go)

    def edge_update(layer):
        def go(rows):
            far = dot(ssrc[rows, nodes:], halo_in[layer]).astype(BF)
            hidden = pre[rows, :] + dot(own[rows, :] + far, ef[layer, 512:1024, :])
            hidden = jnp.maximum(hidden, 0.0).astype(BF)
            update = dot(hidden, es[layer])
            edge[rows, :] = (edge[rows, :].astype(F32) + layer_norm(update)).astype(BF)

        unrolled(edges, go)

    def node_lat_part(layer, h):
        def go(rows):
            hn[rows, :] = dot(h[rows, :], nf[layer, 0:512, :])

        unrolled(nodes, go)

    def mlp(layer, start, first, one, other):
        summed = (one.astype(F32) + other.astype(F32)).astype(BF)
        hidden = jnp.maximum(first + dot(summed, nf[layer, 512:1024, :]), 0.0).astype(BF)
        return (start.astype(F32) + layer_norm(dot(hidden, ns[layer]))).astype(BF)

    def sum_edges(layer, c):
        rows = slice(c * ROWS, (c + 1) * ROWS)
        part[layer, rows, :] = dot(tdst[rows, :], edge[...]).astype(BF)
        exchange(layer, c).start()

    def node_update(layer, h, new):
        for c in range(nodes // ROWS):
            rows = slice(c * ROWS, (c + 1) * ROWS)
            exchange(layer, c).wait_recv()
            new[rows, :] = mlp(layer, h[rows, :], hn[rows, :], part[layer, rows, :], part_in[layer, rows, :])

    loads[1].wait()
    loads[2].wait()
    edge_lat_part(0)
    own_part(0, h0)
    loads[3].wait()
    node_lat_part(0, h0)
    hnh[...] = dot(halo_out[0], nf[0, 0:512, :])
    looped(halos, lambda r: incident(thalo, chalo[pl.ds(r, SEL), :], r))
    looped(nodes, lambda r: incident(tdst, sublanes + r, r))
    index_copy.wait_recv()
    for j in range(requests // 128):
        cprobe[2 * j * 128 : (2 * j + 1) * 128, :] = column(prows_in[j : j + 1, :])
        cprobe[(2 * j + 1) * 128 : (2 * j + 2) * 128, :] = column(prows[j : j + 1, :])
    looped(2 * requests, lambda r: incident(tprobe, cprobe[pl.ds(r, SEL), :], r))
    loads[4].wait()
    loads[5].wait()
    for k in range(8):
        halo_copy(0, k).wait_recv()
    edge_update(0)

    for c in (1, 0):
        rows = slice(c * SEL, (c + 1) * SEL)
        halo_part[rows, :] = dot(thalo[rows, :], edge[...]).astype(BF)
        halo_exchange(c).start()
    sum_edges(0, 0)
    for c in (1, 0):
        rows = slice(c * SEL, (c + 1) * SEL)
        halo_exchange(c).wait_recv()
        halo_out[1, rows, :] = mlp(0, halo_out[0, rows, :], hnh[rows, :], halo_part[rows, :], halo_part_in[rows, :])
        for k in range(4 * c, 4 * c + 4):
            halo_copy(1, k).start()
    sum_edges(0, 1)
    for load in loads[6:]:
        load.wait()
    edge_lat_part(1)
    node_update(0, h0, h1)

    own_part(1, h1)

    def pick_rows(r):
        here = cprobe[pl.ds(2 * r + 128, 128), :]
        for half in range(2):
            here = cprobe[pl.ds(2 * r + 256 * half + 128, 128), :]
            for j in range(nodes // 128):
                hit = jnp.where(here == lanes[0:128] + j * 128, 1.0, 0.0).astype(BF)
                sprobe[pl.ds(r + 128 * half, 128), j * 128 : (j + 1) * 128] = hit

    looped(requests, pick_rows)

    def pick_part(rows):
        picked = dot(sprobe[rows, :], h1[...]).astype(BF)
        pick[rows, :] = picked
        hnp[rows, :] = dot(picked, nf[1, 0:512, :])

    unrolled(requests, pick_part)
    for k in range(8):
        halo_copy(1, k).wait_recv()
    edge_update(1)

    def probe_sums(c):
        here = 4 * qslot * c
        both = dot(tprobe[here : here + 4 * qslot, :], edge[...]).astype(BF)
        for i in range(2):
            rows = slice((2 * c + i) * qslot, (2 * c + i + 1) * qslot)
            theirs[rows, :] = both[2 * i * qslot : (2 * i + 1) * qslot]
            mine[rows, :] = both[(2 * i + 1) * qslot : (2 * i + 2) * qslot]
        probe_exchange(c).start()

    def probe_rows(c):
        rows = slice(2 * c * qslot, (2 * c + 2) * qslot)
        probe_exchange(c).wait_recv()
        probe_out[rows, :] = mlp(1, pick[rows, :], hnp[rows, :], mine[rows, :], theirs_in[rows, :])
        probe_copy(2 * c).start()
        probe_copy(2 * c + 1).start()

    probe_sums(FAR_FIRST[0])
    probe_sums(FAR_FIRST[1])
    probe_rows(FAR_FIRST[0])
    probe_sums(FAR_FIRST[2])
    probe_rows(FAR_FIRST[1])
    probe_sums(FAR_FIRST[3])
    probe_rows(FAR_FIRST[2])
    probe_rows(FAR_FIRST[3])

    sum_edges(1, 0)
    sum_edges(1, 1)
    node_lat_part(1, h1)

    def interp_weights(r):
        here = sublanes + r
        for j in range(probes // 128):
            lane = slice(j * 128, (j + 1) * 128)
            total = jnp.zeros((SEL, 128), F32)
            for s in range(8):
                total = total + jnp.where(here == pslot[s : s + 1, lane], pwgt[s : s + 1, lane], 0.0)
            wint[j * 128 : (j + 1) * 128, pl.ds(r, SEL)] = jnp.transpose(total).astype(BF)

    looped(requests, interp_weights)
    node_update(1, h1, h2)
    store = pltpu.make_async_copy(h2, out_hbm, store_sem.at[0])
    store.start()

    total = emb[...].astype(F32)
    for c in FAR_FIRST:
        rows = slice(2 * c * qslot, (2 * c + 2) * qslot)
        probe_copy(2 * c).wait_recv()
        probe_copy(2 * c + 1).wait_recv()
        total = total + dot(wint[:, rows], probe_in[rows, :])
    hidden = jnp.maximum(dot(total.astype(BF), d1[...]), 0.0).astype(BF)
    fields[...] = lax.dot_general(d2[...], hidden, (((1,), (1,)), ((), ())), preferred_element_type=F32)

    store.wait()
    index_copy.wait_send()
    for k in range(8):
        halo_copy(0, k).wait_send()
        halo_copy(1, k).wait_send()
        probe_copy(k).wait_send()
    for c in range(2):
        exchange(0, c).wait_send()
        exchange(1, c).wait_send()
        halo_exchange(c).wait_send()
    for c in range(4):
        probe_exchange(c).wait_send()


def handover(surface, fields, surface_out, fields_out, rows, line, in_sem, out_sem):
    part = surface.shape[0] // 4
    pieces = [(fields, line, fields_out)]
    for i in range(4):
        cut = pl.ds(i * part, part)
        pieces.append((surface.at[cut, :], rows.at[cut, :], surface_out.at[cut, :]))
    ins = [pltpu.make_async_copy(src, mid, in_sem.at[i]) for i, (src, mid, _) in enumerate(pieces)]
    outs = [pltpu.make_async_copy(mid, dst, out_sem.at[i]) for i, (_, mid, dst) in enumerate(pieces)]
    for move in ins:
        move.start()
    for move, onward in zip(ins, outs):
        move.wait()
        onward.start()
    for onward in outs:
        onward.wait()


def body(
    node_lat, edge_lat, edge_src, edge_dst, halo_rows, probe_rows, probe_slot, probe_wgt, probe_embed,
    edge_first, edge_second, node_first, node_second, decode_first, decode_second,
):
    nodes, width = node_lat.shape
    edges, probes = edge_lat.shape[0], probe_embed.shape[0]
    halos, requests = halo_rows.size, probe_rows.size
    layers, fields = edge_first.shape[0], decode_second.shape[0]
    anywhere = pl.BlockSpec(memory_space=pl.ANY)
    vmem = pl.BlockSpec(memory_space=pltpu.VMEM)
    dma = pltpu.SemaphoreType.DMA
    outs = (
        jax.ShapeDtypeStruct((nodes, width), BF),
        jax.ShapeDtypeStruct((fields, probes), F32),
    )

    def buf(*shape, dtype=BF):
        return pltpu.VMEM(shape, dtype)

    i32 = jnp.int32
    made = pl.pallas_call(
        kernel,
        out_shape=outs,
        in_specs=[anywhere] * 2 + [vmem] * 6 + [anywhere] * 6 + [vmem],
        out_specs=(anywhere, vmem),
        scratch_shapes=[
            buf(nodes, width), buf(nodes, width), buf(nodes, width), buf(edges, width), buf(probes, width),
            buf(*edge_first.shape), buf(*edge_second.shape), buf(*node_first.shape), buf(*node_second.shape),
            buf(*decode_first.shape),
            buf(edges, 128, dtype=i32), buf(edges, 128, dtype=i32), buf(halos, 128, dtype=i32),
            buf(2 * requests, 128, dtype=i32), buf(*probe_rows.shape, dtype=i32),
            buf(edges, nodes + halos), buf(edges, nodes), buf(nodes, edges), buf(halos, nodes), buf(halos, edges),
            buf(requests, nodes), buf(2 * requests, edges), buf(probes, requests),
            buf(edges, width), buf(edges, width, dtype=F32), buf(nodes, width, dtype=F32),
            buf(halos, width, dtype=F32), buf(requests, width, dtype=F32),
            buf(layers, nodes, width), buf(layers, nodes, width), buf(halos, width), buf(halos, width),
            buf(layers, halos, width), buf(layers, halos, width),
            buf(requests, width), buf(requests, width), buf(requests, width), buf(requests, width),
            buf(requests, width), buf(requests, width),
            dma((12,)), dma((1,)), dma((layers, 8)), dma((layers, 8)), dma((layers, 2)), dma((layers, 2)),
            dma((2,)), dma((2,)), dma((4,)), dma((4,)), dma((8,)), dma((8,)), dma((1,)), dma((1,)),
        ],
        compiler_params=pltpu.CompilerParams(
            collective_id=0, has_side_effects=True, vmem_limit_bytes=60 * 1024 * 1024
        ),
    )(
        node_lat, edge_lat, edge_src.reshape(-1, 128), edge_dst.reshape(-1, 128), halo_rows, probe_rows,
        probe_slot.T, probe_wgt.T, probe_embed,
        edge_first, edge_second, node_first, node_second, decode_first, decode_second,
    )
    return pl.pallas_call(
        handover,
        out_shape=outs,
        in_specs=[anywhere] * 2,
        out_specs=(anywhere, anywhere),
        scratch_shapes=[buf(nodes, width), buf(fields, probes, dtype=F32), dma((5,)), dma((5,))],
    )(*made)


def solution(mesh):
    both = P(("dom", "feat"), None)
    return jax.shard_map(
        body,
        mesh=mesh,
        in_specs=(
            P("dom", None), both, P(("dom", "feat")), P(("dom", "feat")), P("dom", None),
            both, both, both, both, P(), P(), P(), P(), P(), P(),
        ),
        out_specs=(P("dom", None), P(None, ("dom", "feat"))),
        check_vma=False,
    )
```

```python
import jax
import jax.numpy as jnp
from jax import lax
from jax.experimental import pallas as pl
from jax.experimental.pallas import tpu as pltpu
from jax.sharding import PartitionSpec as P

SPAN = 4
BF = jnp.bfloat16
F32 = jnp.float32
MESH = pl.DeviceIdType.MESH
OFFSETS = (1, -1, SPAN, -SPAN, SPAN + 1, -SPAN - 1, SPAN - 1, 1 - SPAN)
ROWS = 512
SEL = 256
FAR_FIRST = (2, 3, 0, 1)


def dot(a, b):
    return jnp.dot(a, b, preferred_element_type=F32)


def layer_norm(values):
    centre = jnp.mean(values, axis=-1, keepdims=True)
    shifted = values - centre
    spread = jnp.mean(shifted * shifted, axis=-1, keepdims=True)
    return shifted * lax.rsqrt(spread + 1e-05)


def looped(count, body):
    def step(i, carry):
        body(pl.multiple_of(i * SEL, SEL))
        return carry

    lax.fori_loop(0, count // SEL, step, 0)


def unrolled(count, body):
    for r in range(0, count, ROWS):
        body(slice(r, r + ROWS))


def column(row):
    return jnp.transpose(jnp.broadcast_to(row, (128, 128)))


def kernel(
    node_hbm, edge_hbm, esrc_hbm, edst_hbm, hrows_hbm, prows_hbm, pslot_hbm, pwgt_hbm, emb_hbm,
    ef_hbm, es_hbm, nf_hbm, ns_hbm, d1_hbm, d2_hbm,
    out_hbm, fields,
    esrc, edst, hrows, prows, pslot, pwgt, d2, h0, h1, h2, edge, emb, ef, es, nf, ns, d1,
    csrc, cdst, chalo, cprobe, prows_in, ssrc, sdst, tdst, shalo, thalo, sprobe, tprobe, wint,
    own, pre, hn, hnh, hnp, part, part_in, halo_mine, halo_theirs, halo_theirs_in, halo_out, halo_in,
    pick, mine, theirs, theirs_in, probe_out, probe_in, relay_in,
    load_sem, store_sem, hs_sem, hr_sem, xs_sem, xr_sem, ys_sem, yr_sem, zs_sem, zr_sem, ps_sem, pr_sem, is_sem, ir_sem,
    fs_sem, fr_sem, rs_sem, rr_sem, gs_sem,
):
    nodes, edges = h0.shape[0], edge.shape[0]
    halos, requests, probes = halo_in.shape[1], probe_in.shape[0], emb.shape[0]
    half, hslot, qslot = halos // 2, halos // 16, requests // 8
    count = lax.axis_size("dom")
    dom, feat = lax.axis_index("dom"), lax.axis_index("feat")
    peer = 1 - feat
    targets = [lax.rem(dom + off + count, count) for off in OFFSETS]

    place = lax.rem(dom, SPAN)
    is_first, is_last = place == 0, place == SPAN - 1

    pairs = [
        (hrows_hbm, hrows), (node_hbm, h0),
        (esrc_hbm, esrc), (edst_hbm, edst), (edge_hbm, edge),
        (ef_hbm.at[0], ef.at[0]), (nf_hbm.at[0], nf.at[0]), (prows_hbm, prows),
        (es_hbm.at[0], es.at[0]), (ns_hbm.at[0], ns.at[0]),
        (ef_hbm.at[1], ef.at[1]), (nf_hbm.at[1], nf.at[1]), (es_hbm.at[1], es.at[1]), (ns_hbm.at[1], ns.at[1]),
        (pslot_hbm, pslot), (pwgt_hbm, pwgt), (emb_hbm, emb), (d1_hbm, d1), (d2_hbm, d2),
    ]
    loads = [pltpu.make_async_copy(src, dst, load_sem.at[i]) for i, (src, dst) in enumerate(pairs)]
    loads[0].start()
    loads[1].start()

    barrier = pltpu.get_barrier_semaphore()
    for target in targets:
        pl.semaphore_signal(barrier, inc=1, device_id=(target, feat), device_id_type=MESH)
    pl.semaphore_signal(barrier, inc=1, device_id=(dom, peer), device_id_type=MESH)

    def remote(src, dst, send, recv, device):
        return pltpu.make_async_remote_copy(
            src_ref=src, dst_ref=dst, send_sem=send, recv_sem=recv, device_id=device, device_id_type=MESH
        )

    def halo_copy(layer, k):
        here = pl.ds(k * hslot, hslot)
        there = pl.ds(pl.multiple_of(feat * half + k * hslot, hslot), hslot)
        return remote(halo_out.at[layer, here, :], halo_in.at[layer, there, :],
                      hs_sem.at[layer, k], hr_sem.at[layer, k], (targets[k], feat))

    def halo_share(layer, c):
        rows = pl.ds(pl.multiple_of(feat * half + c * 4 * hslot, 4 * hslot), 4 * hslot)
        return remote(halo_in.at[layer, rows, :], halo_in.at[layer, rows, :],
                      fs_sem.at[layer, c], fr_sem.at[layer, c], (dom, peer))

    def exchange(layer, c):
        rows = pl.ds(c * ROWS, ROWS)
        return remote(part.at[layer, rows, :], part_in.at[layer, rows, :],
                      xs_sem.at[layer, c], xr_sem.at[layer, c], (dom, peer))

    halo_exchange = remote(halo_theirs, halo_theirs_in, ys_sem.at[0], yr_sem.at[0], (dom, peer))

    def probe_exchange(c):
        rows = pl.ds(c * 2 * qslot, 2 * qslot)
        return remote(theirs.at[rows, :], theirs_in.at[rows, :], zs_sem.at[c], zr_sem.at[c], (dom, peer))

    def probe_copy(k):
        rows = pl.ds(k * qslot, qslot)
        return remote(probe_out.at[rows, :], probe_in.at[rows, :], ps_sem.at[k], pr_sem.at[k], (targets[k], feat))

    def relay_out(k):
        rows = pl.ds(k * qslot, qslot)
        return remote(probe_out.at[rows, :], relay_in, rs_sem.at[0], rr_sem.at[0], (targets[k - 4], feat))

    def relay_on(k):
        rows = pl.ds(k * qslot, qslot)
        return remote(relay_in, probe_in.at[rows, :], gs_sem.at[0], pr_sem.at[k], (targets[k - 2], feat))

    relays = ((4, is_last, is_first), (5, is_first, is_last))

    index_copy = remote(prows, prows_in, is_sem.at[0], ir_sem.at[0], (dom, peer))

    lanes = lax.broadcasted_iota(jnp.int32, (SEL, 128), 1)
    sublanes = lax.broadcasted_iota(jnp.int32, (SEL, 128), 0)

    def select(out, col, r):
        here = col[pl.ds(r, SEL), :]
        for j in range(out.shape[1] // 128):
            hit = jnp.where(here == lanes + j * 128, 1.0, 0.0).astype(BF)
            out[pl.ds(r, SEL), j * 128 : (j + 1) * 128] = hit

    def incident(out, here, r):
        for j in range(edges // 128):
            hit = jnp.where(here == edst[j : j + 1, :], 1.0, 0.0).astype(BF)
            out[pl.ds(r, SEL), j * 128 : (j + 1) * 128] = hit

    loads[0].wait()
    for g, core in enumerate((feat, peer)):
        chosen = hrows[:, 0:hslot] + (hrows[:, hslot : 2 * hslot] - hrows[:, 0:hslot]) * core
        for j in range(half // 128):
            row = jnp.concatenate([chosen[k : k + 1, :] for k in range(4 * j, 4 * j + 4)], axis=1)
            chalo[g * half + j * 128 : g * half + (j + 1) * 128, :] = column(row)
    looped(half, lambda r: select(shalo, chalo, r))
    loads[1].wait()
    for load in loads[2:]:
        load.start()
    halo_out[0] = dot(shalo[...], h0[...]).astype(BF)
    pl.semaphore_wait(barrier, 9)
    for k in range(7, -1, -1):
        halo_copy(0, k).start()

    loads[2].wait()
    loads[3].wait()
    bits = hslot.bit_length() - 1
    for j in range(edges // 128):
        sender = esrc[j : j + 1, :]
        far = sender - nodes
        far = ((far >> bits) & 1) * half + (far >> (bits + 1)) * hslot + (far & (hslot - 1))
        csrc[j * 128 : (j + 1) * 128, :] = column(jnp.where(sender < nodes, sender, far + nodes))
        cdst[j * 128 : (j + 1) * 128, :] = column(edst[j : j + 1, :])
    looped(edges, lambda r: (select(ssrc, csrc, r), select(sdst, cdst, r), None)[2])

    def edge_lat_part(layer):
        def go(rows):
            pre[rows, :] = dot(edge[rows, :], ef[layer, 0:512, :])

        unrolled(edges, go)

    def own_part(layer, h):
        def go(rows):
            own[rows, :] = dot(ssrc[rows, 0:nodes], h[...]).astype(BF)
            there = dot(sdst[rows, :], h[...]).astype(BF)
            pre[rows, :] += dot(there, ef[layer, 1024:1536, :])

        unrolled(edges, go)

    def edge_update(layer):
        def go(rows):
            far = dot(ssrc[rows, nodes:], halo_in[layer]).astype(BF)
            hidden = pre[rows, :] + dot(own[rows, :] + far, ef[layer, 512:1024, :])
            hidden = jnp.maximum(hidden, 0.0).astype(BF)
            update = dot(hidden, es[layer])
            edge[rows, :] = (edge[rows, :].astype(F32) + layer_norm(update)).astype(BF)

        unrolled(edges, go)

    def node_lat_part(layer, h):
        def go(rows):
            hn[rows, :] = dot(h[rows, :], nf[layer, 0:512, :])

        unrolled(nodes, go)

    def mlp(layer, start, first, one, other):
        summed = (one.astype(F32) + other.astype(F32)).astype(BF)
        hidden = jnp.maximum(first + dot(summed, nf[layer, 512:1024, :]), 0.0).astype(BF)
        return (start.astype(F32) + layer_norm(dot(hidden, ns[layer]))).astype(BF)

    def sum_edges(layer, c):
        rows = slice(c * ROWS, (c + 1) * ROWS)
        part[layer, rows, :] = dot(tdst[rows, :], edge[...]).astype(BF)
        exchange(layer, c).start()

    def node_update(layer, h, new):
        for c in range(nodes // ROWS):
            rows = slice(c * ROWS, (c + 1) * ROWS)
            exchange(layer, c).wait_recv()
            new[rows, :] = mlp(layer, h[rows, :], hn[rows, :], part[layer, rows, :], part_in[layer, rows, :])

    def share_halo(layer):
        for c in range(2):
            for k in range(4 * c, 4 * c + 4):
                halo_copy(layer, k).wait_recv()
            halo_share(layer, c).start()

    loads[4].wait()
    loads[5].wait()
    edge_lat_part(0)
    own_part(0, h0)
    loads[6].wait()
    node_lat_part(0, h0)
    hnh[...] = dot(halo_out[0], nf[0, 0:512, :])
    looped(halos, lambda r: incident(thalo, chalo[pl.ds(r, SEL), :], r))
    looped(nodes, lambda r: incident(tdst, sublanes + r, r))
    loads[7].wait()
    index_copy.start()
    share_halo(0)
    index_copy.wait_recv()
    for j in range(requests // 128):
        cprobe[2 * j * 128 : (2 * j + 1) * 128, :] = column(prows_in[j : j + 1, :])
        cprobe[(2 * j + 1) * 128 : (2 * j + 2) * 128, :] = column(prows[j : j + 1, :])
    looped(2 * requests, lambda r: incident(tprobe, cprobe[pl.ds(r, SEL), :], r))
    loads[8].wait()
    loads[9].wait()
    for c in range(2):
        halo_share(0, c).wait_recv()
    edge_update(0)

    halo_theirs[...] = dot(thalo[half:, :], edge[...]).astype(BF)
    halo_exchange.start()
    halo_mine[...] = dot(thalo[0:half, :], edge[...]).astype(BF)
    sum_edges(0, 0)
    halo_exchange.wait_recv()
    halo_out[1] = mlp(0, halo_out[0], hnh[...], halo_mine[...], halo_theirs_in[...])
    for k in range(7, -1, -1):
        halo_copy(1, k).start()
    sum_edges(0, 1)
    for load in loads[10:]:
        load.wait()
    edge_lat_part(1)
    node_update(0, h0, h1)

    own_part(1, h1)
    share_halo(1)

    def pick_rows(r):
        for side in range(2):
            here = cprobe[pl.ds(2 * r + 256 * side + 128, 128), :]
            for j in range(nodes // 128):
                hit = jnp.where(here == lanes[0:128] + j * 128, 1.0, 0.0).astype(BF)
                sprobe[pl.ds(r + 128 * side, 128), j * 128 : (j + 1) * 128] = hit

    looped(requests, pick_rows)

    def pick_part(rows):
        picked = dot(sprobe[rows, :], h1[...]).astype(BF)
        pick[rows, :] = picked
        hnp[rows, :] = dot(picked, nf[1, 0:512, :])

    unrolled(requests, pick_part)
    for c in range(2):
        halo_share(1, c).wait_recv()
    edge_update(1)

    def probe_sums(c):
        here = 4 * qslot * c
        both = dot(tprobe[here : here + 4 * qslot, :], edge[...]).astype(BF)
        for i in range(2):
            rows = slice((2 * c + i) * qslot, (2 * c + i + 1) * qslot)
            theirs[rows, :] = both[2 * i * qslot : (2 * i + 1) * qslot]
            mine[rows, :] = both[(2 * i + 1) * qslot : (2 * i + 2) * qslot]
        probe_exchange(c).start()

    def probe_rows(c):
        rows = slice(2 * c * qslot, (2 * c + 2) * qslot)
        probe_exchange(c).wait_recv()
        probe_out[rows, :] = mlp(1, pick[rows, :], hnp[rows, :], mine[rows, :], theirs_in[rows, :])
        if c != 2:
            probe_copy(2 * c).start()
            probe_copy(2 * c + 1).start()
            return
        for k, sends, _ in relays:
            pl.when(sends)(relay_out(k).start)
            pl.when(jnp.logical_not(sends))(probe_copy(k).start)

    probe_sums(FAR_FIRST[0])
    probe_sums(FAR_FIRST[1])
    probe_rows(FAR_FIRST[0])
    probe_sums(FAR_FIRST[2])
    probe_rows(FAR_FIRST[1])
    probe_sums(FAR_FIRST[3])
    probe_rows(FAR_FIRST[2])
    probe_rows(FAR_FIRST[3])

    sum_edges(1, 0)
    sum_edges(1, 1)
    node_lat_part(1, h1)

    def pass_on(k):
        def go():
            relay_out(k).wait_recv()
            relay_on(k).start()

        return go

    for k, _, passes in relays:
        pl.when(passes)(pass_on(k))

    def interp_weights(r):
        here = sublanes + r
        for j in range(probes // 128):
            lane = slice(j * 128, (j + 1) * 128)
            total = jnp.zeros((SEL, 128), F32)
            for s in range(8):
                total = total + jnp.where(here == pslot[s : s + 1, lane], pwgt[s : s + 1, lane], 0.0)
            wint[j * 128 : (j + 1) * 128, pl.ds(r, SEL)] = jnp.transpose(total).astype(BF)

    looped(requests, interp_weights)
    node_update(1, h1, h2)
    store = pltpu.make_async_copy(h2, out_hbm, store_sem.at[0])
    store.start()

    total = emb[...].astype(F32)
    for c in FAR_FIRST:
        rows = slice(2 * c * qslot, (2 * c + 2) * qslot)
        probe_copy(2 * c).wait_recv()
        probe_copy(2 * c + 1).wait_recv()
        total = total + dot(wint[:, rows], probe_in[rows, :])
    hidden = jnp.maximum(dot(total.astype(BF), d1[...]), 0.0).astype(BF)
    fields[...] = lax.dot_general(d2[...], hidden, (((1,), (1,)), ((), ())), preferred_element_type=F32)

    store.wait()
    index_copy.wait_send()
    halo_exchange.wait_send()
    for k in range(8):
        halo_copy(0, k).wait_send()
        halo_copy(1, k).wait_send()
        if k not in (4, 5):
            probe_copy(k).wait_send()
    for k, sends, passes in relays:
        pl.when(sends)(relay_out(k).wait_send)
        pl.when(jnp.logical_not(sends))(probe_copy(k).wait_send)
        pl.when(passes)(relay_on(k).wait_send)
    for c in range(2):
        for layer in range(2):
            exchange(layer, c).wait_send()
            halo_share(layer, c).wait_send()
    for c in range(4):
        probe_exchange(c).wait_send()


def handover(surface, fields, surface_out, fields_out, rows, line, in_sem, out_sem):
    part = surface.shape[0] // 4
    pieces = [(fields, line, fields_out)]
    for i in range(4):
        cut = pl.ds(i * part, part)
        pieces.append((surface.at[cut, :], rows.at[cut, :], surface_out.at[cut, :]))
    ins = [pltpu.make_async_copy(src, mid, in_sem.at[i]) for i, (src, mid, _) in enumerate(pieces)]
    outs = [pltpu.make_async_copy(mid, dst, out_sem.at[i]) for i, (_, mid, dst) in enumerate(pieces)]
    for move in ins:
        move.start()
    for move, onward in zip(ins, outs):
        move.wait()
        onward.start()
    for onward in outs:
        onward.wait()


def body(
    node_lat, edge_lat, edge_src, edge_dst, halo_rows, probe_rows, probe_slot, probe_wgt, probe_embed,
    edge_first, edge_second, node_first, node_second, decode_first, decode_second,
):
    nodes, width = node_lat.shape
    edges, probes = edge_lat.shape[0], probe_embed.shape[0]
    halos, requests = halo_rows.size, probe_rows.size
    layers, fields = edge_first.shape[0], decode_second.shape[0]
    anywhere = pl.BlockSpec(memory_space=pl.ANY)
    vmem = pl.BlockSpec(memory_space=pltpu.VMEM)
    dma = pltpu.SemaphoreType.DMA
    outs = (
        jax.ShapeDtypeStruct((nodes, width), BF),
        jax.ShapeDtypeStruct((fields, probes), F32),
    )

    def buf(*shape, dtype=BF):
        return pltpu.VMEM(shape, dtype)

    i32 = jnp.int32
    made = pl.pallas_call(
        kernel,
        out_shape=outs,
        in_specs=[anywhere] * 15,
        out_specs=(anywhere, vmem),
        scratch_shapes=[
            buf(edges // 128, 128, dtype=i32), buf(edges // 128, 128, dtype=i32),
            buf(*halo_rows.shape, dtype=i32), buf(*probe_rows.shape, dtype=i32),
            buf(*probe_slot.shape[::-1], dtype=i32), buf(*probe_wgt.shape[::-1], dtype=F32), buf(*decode_second.shape),
            buf(nodes, width), buf(nodes, width), buf(nodes, width), buf(edges, width), buf(probes, width),
            buf(*edge_first.shape), buf(*edge_second.shape), buf(*node_first.shape), buf(*node_second.shape),
            buf(*decode_first.shape),
            buf(edges, 128, dtype=i32), buf(edges, 128, dtype=i32), buf(halos, 128, dtype=i32),
            buf(2 * requests, 128, dtype=i32), buf(*probe_rows.shape, dtype=i32),
            buf(edges, nodes + halos), buf(edges, nodes), buf(nodes, edges), buf(halos // 2, nodes), buf(halos, edges),
            buf(requests, nodes), buf(2 * requests, edges), buf(probes, requests),
            buf(edges, width), buf(edges, width, dtype=F32), buf(nodes, width, dtype=F32),
            buf(halos // 2, width, dtype=F32), buf(requests, width, dtype=F32),
            buf(layers, nodes, width), buf(layers, nodes, width),
            buf(halos // 2, width), buf(halos // 2, width), buf(halos // 2, width),
            buf(layers, halos // 2, width), buf(layers, halos, width),
            buf(requests, width), buf(requests, width), buf(requests, width), buf(requests, width),
            buf(requests, width), buf(requests, width), buf(requests // 8, width),
            dma((19,)), dma((1,)), dma((layers, 8)), dma((layers, 8)), dma((layers, 2)), dma((layers, 2)),
            dma((1,)), dma((1,)), dma((4,)), dma((4,)), dma((8,)), dma((8,)), dma((1,)), dma((1,)),
            dma((layers, 2)), dma((layers, 2)), dma((1,)), dma((1,)), dma((1,)),
        ],
        compiler_params=pltpu.CompilerParams(
            collective_id=0, has_side_effects=True, vmem_limit_bytes=60 * 1024 * 1024
        ),
    )(
        node_lat, edge_lat, edge_src.reshape(-1, 128), edge_dst.reshape(-1, 128), halo_rows, probe_rows,
        probe_slot.T, probe_wgt.T, probe_embed,
        edge_first, edge_second, node_first, node_second, decode_first, decode_second,
    )
    return pl.pallas_call(
        handover,
        out_shape=outs,
        in_specs=[anywhere] * 2,
        out_specs=(anywhere, anywhere),
        scratch_shapes=[buf(nodes, width), buf(fields, probes, dtype=F32), dma((5,)), dma((5,))],
    )(*made)


def solution(mesh):
    both = P(("dom", "feat"), None)
    return jax.shard_map(
        body,
        mesh=mesh,
        in_specs=(
            P("dom", None), both, P(("dom", "feat")), P(("dom", "feat")), P("dom", None),
            both, both, both, both, P(), P(), P(), P(), P(), P(),
        ),
        out_specs=(P("dom", None), P(None, ("dom", "feat"))),
        check_vma=False,
    )
```

```python
import jax
import jax.numpy as jnp
from jax import lax
from jax.experimental import pallas as pl
from jax.experimental.pallas import tpu as pltpu
from jax.sharding import PartitionSpec as P

SPAN = 4
BF = jnp.bfloat16
F32 = jnp.float32
MESH = pl.DeviceIdType.MESH
OFFSETS = (1, -1, SPAN, -SPAN, SPAN + 1, -SPAN - 1, SPAN - 1, 1 - SPAN)
ROWS = 512
SEL = 256
PIECES = ((4, 1), (5, 1), (0, 2), (6, 2), (2, 2))


def dot(a, b):
    return jnp.dot(a, b, preferred_element_type=F32)


def layer_norm(values):
    centre = jnp.mean(values, axis=-1, keepdims=True)
    shifted = values - centre
    spread = jnp.mean(shifted * shifted, axis=-1, keepdims=True)
    return shifted * lax.rsqrt(spread + 1e-05)


def looped(count, body):
    def step(i, carry):
        body(pl.multiple_of(i * SEL, SEL))
        return carry

    lax.fori_loop(0, count // SEL, step, 0)


def unrolled(count, body):
    for r in range(0, count, ROWS):
        body(slice(r, r + ROWS))


def column(row):
    return jnp.transpose(jnp.broadcast_to(row, (128, 128)))


def kernel(
    node_hbm, edge_hbm, esrc_hbm, edst_hbm, hrows_hbm, prows_hbm, pslot_hbm, pwgt_hbm, emb_hbm,
    ef_hbm, es_hbm, nf_hbm, ns_hbm, d1_hbm, d2_hbm,
    out_hbm, fields,
    esrc, edst, hrows, prows, pslot, pwgt, d2, h0, h1, h2, edge, emb, ef, es, nf, ns, d1,
    csrc, cdst, chalo, cprobe, prows_in, ssrc, sdst, tdst, shalo, thalo, sprobe, tprobe, wint,
    own, pre, hn, hnh, hnp, part, part_in, halo_mine, halo_theirs, halo_theirs_in, halo_out, halo_in,
    pick, mine, theirs, theirs_in, probe_out, probe_in, relay_in,
    load_sem, store_sem, hs_sem, hr_sem, xs_sem, xr_sem, ys_sem, yr_sem, zs_sem, zr_sem, ps_sem, pr_sem, is_sem, ir_sem,
    fs_sem, fr_sem, rs_sem, rr_sem, gs_sem,
):
    nodes, edges = h0.shape[0], edge.shape[0]
    halos, requests, probes = halo_in.shape[1], probe_in.shape[0], emb.shape[0]
    half, hslot, qslot = halos // 2, halos // 16, requests // 8
    count = lax.axis_size("dom")
    dom, feat = lax.axis_index("dom"), lax.axis_index("feat")
    peer = 1 - feat
    targets = [lax.rem(dom + off + count, count) for off in OFFSETS]

    place = lax.rem(dom, SPAN)
    is_first, is_last = place == 0, place == SPAN - 1

    pairs = [
        (hrows_hbm, hrows), (node_hbm, h0),
        (esrc_hbm, esrc), (edst_hbm, edst), (edge_hbm, edge),
        (ef_hbm.at[0], ef.at[0]), (nf_hbm.at[0], nf.at[0]), (prows_hbm, prows),
        (es_hbm.at[0], es.at[0]), (ns_hbm.at[0], ns.at[0]),
        (ef_hbm.at[1], ef.at[1]), (nf_hbm.at[1], nf.at[1]), (es_hbm.at[1], es.at[1]), (ns_hbm.at[1], ns.at[1]),
        (pslot_hbm, pslot), (pwgt_hbm, pwgt), (emb_hbm, emb), (d1_hbm, d1), (d2_hbm, d2),
    ]
    loads = [pltpu.make_async_copy(src, dst, load_sem.at[i]) for i, (src, dst) in enumerate(pairs)]
    loads[0].start()
    loads[1].start()

    barrier = pltpu.get_barrier_semaphore()
    for target in targets:
        pl.semaphore_signal(barrier, inc=1, device_id=(target, feat), device_id_type=MESH)
    pl.semaphore_signal(barrier, inc=1, device_id=(dom, peer), device_id_type=MESH)

    def remote(src, dst, send, recv, device):
        return pltpu.make_async_remote_copy(
            src_ref=src, dst_ref=dst, send_sem=send, recv_sem=recv, device_id=device, device_id_type=MESH
        )

    def halo_copy(layer, k):
        here = pl.ds(k * hslot, hslot)
        there = pl.ds(pl.multiple_of(feat * half + k * hslot, hslot), hslot)
        return remote(halo_out.at[layer, here, :], halo_in.at[layer, there, :],
                      hs_sem.at[layer, k], hr_sem.at[layer, k], (targets[k], feat))

    def halo_share(layer, c):
        rows = pl.ds(pl.multiple_of(feat * half + c * 4 * hslot, 4 * hslot), 4 * hslot)
        return remote(halo_in.at[layer, rows, :], halo_in.at[layer, rows, :],
                      fs_sem.at[layer, c], fr_sem.at[layer, c], (dom, peer))

    def exchange(layer, c):
        rows = pl.ds(c * ROWS, ROWS)
        return remote(part.at[layer, rows, :], part_in.at[layer, rows, :],
                      xs_sem.at[layer, c], xr_sem.at[layer, c], (dom, peer))

    halo_exchange = remote(halo_theirs, halo_theirs_in, ys_sem.at[0], yr_sem.at[0], (dom, peer))

    def probe_exchange(i):
        rows = pl.ds(PIECES[i][0] * qslot, PIECES[i][1] * qslot)
        return remote(theirs.at[rows, :], theirs_in.at[rows, :], zs_sem.at[i], zr_sem.at[i], (dom, peer))

    def probe_copy(k):
        rows = pl.ds(k * qslot, qslot)
        return remote(probe_out.at[rows, :], probe_in.at[rows, :], ps_sem.at[k], pr_sem.at[k], (targets[k], feat))

    even = feat == 0
    relays = (
        (4, is_last, is_first, 0, 2, 0),
        (5, is_first, is_last, 1, 3, 0),
        (0, jnp.logical_and(is_last, even), jnp.logical_and(is_first, even), 7, 2, 1),
        (1, jnp.logical_and(is_first, even), jnp.logical_and(is_last, even), 6, 3, 1),
    )

    def relay_out(k, via, i):
        rows = pl.ds(k * qslot, qslot)
        return remote(probe_out.at[rows, :], relay_in.at[i], rs_sem.at[i], rr_sem.at[i], (targets[via], feat))

    def relay_on(k, on, i):
        rows = pl.ds(k * qslot, qslot)
        return remote(relay_in.at[i], probe_in.at[rows, :], gs_sem.at[i], pr_sem.at[k], (targets[on], feat))

    def pass_on(buffer):
        for k, _, passes, via, on, i in relays:
            if i == buffer:

                @pl.when(passes)
                def _():
                    relay_out(k, via, i).wait_recv()
                    relay_on(k, on, i).start()

    index_copy = remote(prows, prows_in, is_sem.at[0], ir_sem.at[0], (dom, peer))

    lanes = lax.broadcasted_iota(jnp.int32, (SEL, 128), 1)
    sublanes = lax.broadcasted_iota(jnp.int32, (SEL, 128), 0)

    def select(out, col, r):
        here = col[pl.ds(r, SEL), :]
        for j in range(out.shape[1] // 128):
            hit = jnp.where(here == lanes + j * 128, 1.0, 0.0).astype(BF)
            out[pl.ds(r, SEL), j * 128 : (j + 1) * 128] = hit

    def incident(out, here, r):
        for j in range(edges // 128):
            hit = jnp.where(here == edst[j : j + 1, :], 1.0, 0.0).astype(BF)
            out[pl.ds(r, SEL), j * 128 : (j + 1) * 128] = hit

    loads[0].wait()
    for g, core in enumerate((feat, peer)):
        chosen = hrows[:, 0:hslot] + (hrows[:, hslot : 2 * hslot] - hrows[:, 0:hslot]) * core
        for j in range(half // 128):
            row = jnp.concatenate([chosen[k : k + 1, :] for k in range(4 * j, 4 * j + 4)], axis=1)
            chalo[g * half + j * 128 : g * half + (j + 1) * 128, :] = column(row)
    looped(half, lambda r: select(shalo, chalo, r))
    loads[1].wait()
    for load in loads[2:]:
        load.start()
    halo_out[0] = dot(shalo[...], h0[...]).astype(BF)
    pl.semaphore_wait(barrier, 9)
    for k in range(7, -1, -1):
        halo_copy(0, k).start()

    loads[2].wait()
    loads[3].wait()
    bits = hslot.bit_length() - 1
    for j in range(edges // 128):
        sender = esrc[j : j + 1, :]
        far = sender - nodes
        far = ((far >> bits) & 1) * half + (far >> (bits + 1)) * hslot + (far & (hslot - 1))
        csrc[j * 128 : (j + 1) * 128, :] = column(jnp.where(sender < nodes, sender, far + nodes))
        cdst[j * 128 : (j + 1) * 128, :] = column(edst[j : j + 1, :])
    looped(edges, lambda r: (select(ssrc, csrc, r), select(sdst, cdst, r), None)[2])

    def edge_lat_part(layer):
        def go(rows):
            pre[rows, :] = dot(edge[rows, :], ef[layer, 0:512, :])

        unrolled(edges, go)

    def own_part(layer, h):
        def go(rows):
            own[rows, :] = dot(ssrc[rows, 0:nodes], h[...]).astype(BF)
            there = dot(sdst[rows, :], h[...]).astype(BF)
            pre[rows, :] += dot(there, ef[layer, 1024:1536, :])

        unrolled(edges, go)

    def edge_update(layer):
        def go(rows):
            far = dot(ssrc[rows, nodes:], halo_in[layer]).astype(BF)
            hidden = pre[rows, :] + dot(own[rows, :] + far, ef[layer, 512:1024, :])
            hidden = jnp.maximum(hidden, 0.0).astype(BF)
            update = dot(hidden, es[layer])
            edge[rows, :] = (edge[rows, :].astype(F32) + layer_norm(update)).astype(BF)

        unrolled(edges, go)

    def node_lat_part(layer, h):
        def go(rows):
            hn[rows, :] = dot(h[rows, :], nf[layer, 0:512, :])

        unrolled(nodes, go)

    def mlp(layer, start, first, one, other):
        summed = (one.astype(F32) + other.astype(F32)).astype(BF)
        hidden = jnp.maximum(first + dot(summed, nf[layer, 512:1024, :]), 0.0).astype(BF)
        return (start.astype(F32) + layer_norm(dot(hidden, ns[layer]))).astype(BF)

    def sum_edges(layer, c):
        rows = slice(c * ROWS, (c + 1) * ROWS)
        part[layer, rows, :] = dot(tdst[rows, :], edge[...]).astype(BF)
        exchange(layer, c).start()

    def node_update(layer, h, new, c):
        rows = slice(c * ROWS, (c + 1) * ROWS)
        exchange(layer, c).wait_recv()
        new[rows, :] = mlp(layer, h[rows, :], hn[rows, :], part[layer, rows, :], part_in[layer, rows, :])

    def share_halo(layer):
        for c in range(2):
            for k in range(4 * c, 4 * c + 4):
                halo_copy(layer, k).wait_recv()
            halo_share(layer, c).start()

    loads[4].wait()
    loads[5].wait()
    edge_lat_part(0)
    own_part(0, h0)
    loads[6].wait()
    node_lat_part(0, h0)
    hnh[...] = dot(halo_out[0], nf[0, 0:512, :])
    looped(halos, lambda r: incident(thalo, chalo[pl.ds(r, SEL), :], r))
    looped(nodes, lambda r: incident(tdst, sublanes + r, r))
    loads[7].wait()
    index_copy.start()
    share_halo(0)
    index_copy.wait_recv()
    for j in range(requests // 128):
        cprobe[2 * j * 128 : (2 * j + 1) * 128, :] = column(prows_in[j : j + 1, :])
        cprobe[(2 * j + 1) * 128 : (2 * j + 2) * 128, :] = column(prows[j : j + 1, :])
    looped(2 * requests, lambda r: incident(tprobe, cprobe[pl.ds(r, SEL), :], r))
    loads[8].wait()
    loads[9].wait()
    for c in range(2):
        halo_share(0, c).wait_recv()
    edge_update(0)

    halo_theirs[...] = dot(thalo[half:, :], edge[...]).astype(BF)
    halo_exchange.start()
    halo_mine[...] = dot(thalo[0:half, :], edge[...]).astype(BF)
    sum_edges(0, 0)
    halo_exchange.wait_recv()
    halo_out[1] = mlp(0, halo_out[0], hnh[...], halo_mine[...], halo_theirs_in[...])
    for k in range(7, -1, -1):
        halo_copy(1, k).start()
    sum_edges(0, 1)
    for load in loads[10:]:
        load.wait()
    edge_lat_part(1)
    node_update(0, h0, h1, 0)

    def pick_rows(r):
        for side in range(2):
            here = cprobe[pl.ds(2 * r + 256 * side + 128, 128), :]
            for j in range(nodes // 128):
                hit = jnp.where(here == lanes[0:128] + j * 128, 1.0, 0.0).astype(BF)
                sprobe[pl.ds(r + 128 * side, 128), j * 128 : (j + 1) * 128] = hit

    looped(requests, pick_rows)
    node_update(0, h0, h1, 1)

    own_part(1, h1)
    share_halo(1)

    def pick_part(rows):
        picked = dot(sprobe[rows, :], h1[...]).astype(BF)
        pick[rows, :] = picked
        hnp[rows, :] = dot(picked, nf[1, 0:512, :])

    pick_part(slice(4 * qslot, 6 * qslot))
    pick_part(slice(0, 4 * qslot))
    for c in range(2):
        halo_share(1, c).wait_recv()
    edge_update(1)

    def probe_sums(i):
        first, number = PIECES[i]
        both = dot(tprobe[2 * first * qslot : 2 * (first + number) * qslot, :], edge[...]).astype(BF)
        for n in range(number):
            rows = slice((first + n) * qslot, (first + n + 1) * qslot)
            theirs[rows, :] = both[2 * n * qslot : (2 * n + 1) * qslot]
            mine[rows, :] = both[(2 * n + 1) * qslot : (2 * n + 2) * qslot]
        probe_exchange(i).start()

    def probe_rows(i):
        first, number = PIECES[i]
        rows = slice(first * qslot, (first + number) * qslot)
        probe_exchange(i).wait_recv()
        probe_out[rows, :] = mlp(1, pick[rows, :], hnp[rows, :], mine[rows, :], theirs_in[rows, :])
        for k in range(first, first + number):
            relayed = [relay for relay in relays if relay[0] == k]
            for _, sends, _, via, _, i in relayed:
                pl.when(sends)(relay_out(k, via, i).start)
                pl.when(jnp.logical_not(sends))(probe_copy(k).start)
            if not relayed:
                probe_copy(k).start()

    probe_sums(0)
    probe_sums(1)
    probe_sums(2)
    probe_rows(0)
    probe_rows(1)
    probe_sums(3)
    probe_rows(2)
    pick_part(slice(6 * qslot, 8 * qslot))
    probe_sums(4)
    probe_rows(3)
    probe_rows(4)
    pass_on(0)

    sum_edges(1, 0)
    sum_edges(1, 1)
    node_lat_part(1, h1)

    pass_on(1)

    def interp_weights(r):
        here = sublanes + r
        for j in range(probes // 128):
            lane = slice(j * 128, (j + 1) * 128)
            total = jnp.zeros((SEL, 128), F32)
            for s in range(8):
                total = total + jnp.where(here == pslot[s : s + 1, lane], pwgt[s : s + 1, lane], 0.0)
            wint[j * 128 : (j + 1) * 128, pl.ds(r, SEL)] = jnp.transpose(total).astype(BF)

    looped(requests, interp_weights)
    node_update(1, h1, h2, 0)
    node_update(1, h1, h2, 1)
    store = pltpu.make_async_copy(h2, out_hbm, store_sem.at[0])
    store.start()

    total = emb[...].astype(F32)
    for c in (1, 3, 0, 2):
        rows = slice(2 * c * qslot, (2 * c + 2) * qslot)
        probe_copy(2 * c).wait_recv()
        probe_copy(2 * c + 1).wait_recv()
        total = total + dot(wint[:, rows], probe_in[rows, :])
    hidden = jnp.maximum(dot(total.astype(BF), d1[...]), 0.0).astype(BF)
    fields[...] = lax.dot_general(d2[...], hidden, (((1,), (1,)), ((), ())), preferred_element_type=F32)

    store.wait()
    index_copy.wait_send()
    halo_exchange.wait_send()
    for k in range(8):
        halo_copy(0, k).wait_send()
        halo_copy(1, k).wait_send()
        relayed = [relay for relay in relays if relay[0] == k]
        for _, sends, passes, via, on, i in relayed:
            pl.when(sends)(relay_out(k, via, i).wait_send)
            pl.when(jnp.logical_not(sends))(probe_copy(k).wait_send)
            pl.when(passes)(relay_on(k, on, i).wait_send)
        if not relayed:
            probe_copy(k).wait_send()
    for c in range(2):
        for layer in range(2):
            exchange(layer, c).wait_send()
            halo_share(layer, c).wait_send()
    for i in range(len(PIECES)):
        probe_exchange(i).wait_send()


def handover(surface, fields, surface_out, fields_out, rows, line, in_sem, out_sem):
    part = surface.shape[0] // 8
    pieces = [(fields, line, fields_out)]
    for i in range(8):
        cut = pl.ds(i * part, part)
        pieces.append((surface.at[cut, :], rows.at[cut, :], surface_out.at[cut, :]))
    ins = [pltpu.make_async_copy(src, mid, in_sem.at[i]) for i, (src, mid, _) in enumerate(pieces)]
    outs = [pltpu.make_async_copy(mid, dst, out_sem.at[i]) for i, (_, mid, dst) in enumerate(pieces)]
    for move in ins:
        move.start()
    for move, onward in zip(ins, outs):
        move.wait()
        onward.start()
    for onward in outs:
        onward.wait()


def body(
    node_lat, edge_lat, edge_src, edge_dst, halo_rows, probe_rows, probe_slot, probe_wgt, probe_embed,
    edge_first, edge_second, node_first, node_second, decode_first, decode_second,
):
    nodes, width = node_lat.shape
    edges, probes = edge_lat.shape[0], probe_embed.shape[0]
    halos, requests = halo_rows.size, probe_rows.size
    layers, fields = edge_first.shape[0], decode_second.shape[0]
    anywhere = pl.BlockSpec(memory_space=pl.ANY)
    vmem = pl.BlockSpec(memory_space=pltpu.VMEM)
    dma = pltpu.SemaphoreType.DMA
    outs = (
        jax.ShapeDtypeStruct((nodes, width), BF),
        jax.ShapeDtypeStruct((fields, probes), F32),
    )

    def buf(*shape, dtype=BF):
        return pltpu.VMEM(shape, dtype)

    i32 = jnp.int32
    made = pl.pallas_call(
        kernel,
        out_shape=outs,
        in_specs=[anywhere] * 15,
        out_specs=(anywhere, vmem),
        scratch_shapes=[
            buf(edges // 128, 128, dtype=i32), buf(edges // 128, 128, dtype=i32),
            buf(*halo_rows.shape, dtype=i32), buf(*probe_rows.shape, dtype=i32),
            buf(*probe_slot.shape[::-1], dtype=i32), buf(*probe_wgt.shape[::-1], dtype=F32), buf(*decode_second.shape),
            buf(nodes, width), buf(nodes, width), buf(nodes, width), buf(edges, width), buf(probes, width),
            buf(*edge_first.shape), buf(*edge_second.shape), buf(*node_first.shape), buf(*node_second.shape),
            buf(*decode_first.shape),
            buf(edges, 128, dtype=i32), buf(edges, 128, dtype=i32), buf(halos, 128, dtype=i32),
            buf(2 * requests, 128, dtype=i32), buf(*probe_rows.shape, dtype=i32),
            buf(edges, nodes + halos), buf(edges, nodes), buf(nodes, edges), buf(halos // 2, nodes), buf(halos, edges),
            buf(requests, nodes), buf(2 * requests, edges), buf(probes, requests),
            buf(edges, width), buf(edges, width, dtype=F32), buf(nodes, width, dtype=F32),
            buf(halos // 2, width, dtype=F32), buf(requests, width, dtype=F32),
            buf(layers, nodes, width), buf(layers, nodes, width),
            buf(halos // 2, width), buf(halos // 2, width), buf(halos // 2, width),
            buf(layers, halos // 2, width), buf(layers, halos, width),
            buf(requests, width), buf(requests, width), buf(requests, width), buf(requests, width),
            buf(requests, width), buf(requests, width), buf(2, requests // 8, width),
            dma((19,)), dma((1,)), dma((layers, 8)), dma((layers, 8)), dma((layers, 2)), dma((layers, 2)),
            dma((1,)), dma((1,)), dma((5,)), dma((5,)), dma((8,)), dma((8,)), dma((1,)), dma((1,)),
            dma((layers, 2)), dma((layers, 2)), dma((2,)), dma((2,)), dma((2,)),
        ],
        compiler_params=pltpu.CompilerParams(
            collective_id=0, has_side_effects=True, vmem_limit_bytes=60 * 1024 * 1024
        ),
    )(
        node_lat, edge_lat, edge_src.reshape(-1, 128), edge_dst.reshape(-1, 128), halo_rows, probe_rows,
        probe_slot.T, probe_wgt.T, probe_embed,
        edge_first, edge_second, node_first, node_second, decode_first, decode_second,
    )
    return pl.pallas_call(
        handover,
        out_shape=outs,
        in_specs=[anywhere] * 2,
        out_specs=(anywhere, anywhere),
        scratch_shapes=[buf(nodes, width), buf(fields, probes, dtype=F32), dma((9,)), dma((9,))],
    )(*made)


def solution(mesh):
    both = P(("dom", "feat"), None)
    return jax.shard_map(
        body,
        mesh=mesh,
        in_specs=(
            P("dom", None), both, P(("dom", "feat")), P(("dom", "feat")), P("dom", None),
            both, both, both, both, P(), P(), P(), P(), P(), P(),
        ),
        out_specs=(P("dom", None), P(None, ("dom", "feat"))),
        check_vma=False,
    )
```

```python
import jax
import jax.numpy as jnp
from jax import lax
from jax.experimental import pallas as pl
from jax.experimental.pallas import tpu as pltpu
from jax.sharding import PartitionSpec as P

SPAN = 4
BF = jnp.bfloat16
F32 = jnp.float32
MESH = pl.DeviceIdType.MESH
OFFSETS = (1, -1, SPAN, -SPAN, SPAN + 1, -SPAN - 1, SPAN - 1, 1 - SPAN)
ROWS = 512
SEL = 256
PIECES = ((4, 1), (5, 1), (0, 2), (6, 2), (2, 2))


def dot(a, b):
    return jnp.dot(a, b, preferred_element_type=F32)


def layer_norm(values):
    centre = jnp.mean(values, axis=-1, keepdims=True)
    shifted = values - centre
    spread = jnp.mean(shifted * shifted, axis=-1, keepdims=True)
    return shifted * lax.rsqrt(spread + 1e-05)


def looped(count, body):
    def step(i, carry):
        body(pl.multiple_of(i * SEL, SEL))
        return carry

    lax.fori_loop(0, count // SEL, step, 0)


def unrolled(count, body):
    for r in range(0, count, ROWS):
        body(slice(r, r + ROWS))


def column(row):
    return jnp.transpose(jnp.broadcast_to(row, (128, 128)))


def kernel(
    node_hbm, edge_hbm, esrc_hbm, edst_hbm, hrows_hbm, prows_hbm, pslot_hbm, pwgt_hbm, emb_hbm,
    ef_hbm, es_hbm, nf_hbm, ns_hbm, d1_hbm, d2_hbm,
    h2, fields,
    esrc, edst, hrows, prows, pslot, pwgt, d2, h0, h1, edge, emb, ef, es, nf, ns, d1,
    csrc, cdst, chalo, cprobe, prows_in, ssrc, sdst, tdst, shalo, thalo, sprobe, tprobe, wint,
    own, pre, hn, hnh, hnp, part, part_in, halo_mine, halo_theirs, halo_theirs_in, halo_out, halo_in,
    pick, mine, theirs, theirs_in, probe_out, probe_in, relay_in,
    load_sem, hs_sem, hr_sem, xs_sem, xr_sem, ys_sem, yr_sem, zs_sem, zr_sem, ps_sem, pr_sem, is_sem, ir_sem,
    fs_sem, fr_sem, rs_sem, rr_sem, gs_sem,
):
    nodes, edges = h0.shape[0], edge.shape[0]
    halos, requests, probes = halo_in.shape[1], probe_in.shape[0], emb.shape[0]
    half, hslot, qslot = halos // 2, halos // 16, requests // 8
    count = lax.axis_size("dom")
    dom, feat = lax.axis_index("dom"), lax.axis_index("feat")
    peer = 1 - feat
    targets = [lax.rem(dom + off + count, count) for off in OFFSETS]

    place = lax.rem(dom, SPAN)
    is_first, is_last = place == 0, place == SPAN - 1

    pairs = [
        (hrows_hbm, hrows), (node_hbm, h0),
        (esrc_hbm, esrc), (edst_hbm, edst), (edge_hbm, edge),
        (ef_hbm.at[0], ef.at[0]), (nf_hbm.at[0], nf.at[0]), (prows_hbm, prows),
        (es_hbm.at[0], es.at[0]), (ns_hbm.at[0], ns.at[0]),
        (ef_hbm.at[1], ef.at[1]), (nf_hbm.at[1], nf.at[1]), (es_hbm.at[1], es.at[1]), (ns_hbm.at[1], ns.at[1]),
        (pslot_hbm, pslot), (pwgt_hbm, pwgt), (emb_hbm, emb), (d1_hbm, d1), (d2_hbm, d2),
    ]
    loads = [pltpu.make_async_copy(src, dst, load_sem.at[i]) for i, (src, dst) in enumerate(pairs)]
    loads[0].start()
    loads[1].start()

    barrier = pltpu.get_barrier_semaphore()
    for target in targets:
        pl.semaphore_signal(barrier, inc=1, device_id=(target, feat), device_id_type=MESH)
    pl.semaphore_signal(barrier, inc=1, device_id=(dom, peer), device_id_type=MESH)

    def remote(src, dst, send, recv, device):
        return pltpu.make_async_remote_copy(
            src_ref=src, dst_ref=dst, send_sem=send, recv_sem=recv, device_id=device, device_id_type=MESH
        )

    def halo_copy(layer, k):
        here = pl.ds(k * hslot, hslot)
        there = pl.ds(pl.multiple_of(feat * half + k * hslot, hslot), hslot)
        return remote(halo_out.at[layer, here, :], halo_in.at[layer, there, :],
                      hs_sem.at[layer, k], hr_sem.at[layer, k], (targets[k], feat))

    def halo_share(layer, c):
        rows = pl.ds(pl.multiple_of(feat * half + c * 4 * hslot, 4 * hslot), 4 * hslot)
        return remote(halo_in.at[layer, rows, :], halo_in.at[layer, rows, :],
                      fs_sem.at[layer, c], fr_sem.at[layer, c], (dom, peer))

    def exchange(layer, c):
        rows = pl.ds(c * ROWS, ROWS)
        return remote(part.at[layer, rows, :], part_in.at[layer, rows, :],
                      xs_sem.at[layer, c], xr_sem.at[layer, c], (dom, peer))

    halo_exchange = remote(halo_theirs, halo_theirs_in, ys_sem.at[0], yr_sem.at[0], (dom, peer))

    def probe_exchange(i):
        rows = pl.ds(PIECES[i][0] * qslot, PIECES[i][1] * qslot)
        return remote(theirs.at[rows, :], theirs_in.at[rows, :], zs_sem.at[i], zr_sem.at[i], (dom, peer))

    def probe_copy(k):
        rows = pl.ds(k * qslot, qslot)
        return remote(probe_out.at[rows, :], probe_in.at[rows, :], ps_sem.at[k], pr_sem.at[k], (targets[k], feat))

    even = feat == 0
    relays = (
        (4, is_last, is_first, 0, 2, 0),
        (5, is_first, is_last, 1, 3, 0),
    )

    def relay_out(k, via, i):
        rows = pl.ds(k * qslot, qslot)
        return remote(probe_out.at[rows, :], relay_in.at[i], rs_sem.at[i], rr_sem.at[i], (targets[via], feat))

    def relay_on(k, on, i):
        rows = pl.ds(k * qslot, qslot)
        return remote(relay_in.at[i], probe_in.at[rows, :], gs_sem.at[i], pr_sem.at[k], (targets[on], feat))

    def pass_on(buffer):
        for k, _, passes, via, on, i in relays:
            if i == buffer:

                @pl.when(passes)
                def _():
                    relay_out(k, via, i).wait_recv()
                    relay_on(k, on, i).start()

    index_copy = remote(prows, prows_in, is_sem.at[0], ir_sem.at[0], (dom, peer))

    lanes = lax.broadcasted_iota(jnp.int32, (SEL, 128), 1)
    sublanes = lax.broadcasted_iota(jnp.int32, (SEL, 128), 0)

    def select(out, col, r):
        here = col[pl.ds(r, SEL), :]
        for j in range(out.shape[1] // 128):
            hit = jnp.where(here == lanes + j * 128, 1.0, 0.0).astype(BF)
            out[pl.ds(r, SEL), j * 128 : (j + 1) * 128] = hit

    def incident(out, here, r):
        for j in range(edges // 128):
            hit = jnp.where(here == edst[j : j + 1, :], 1.0, 0.0).astype(BF)
            out[pl.ds(r, SEL), j * 128 : (j + 1) * 128] = hit

    loads[0].wait()
    for g, core in enumerate((feat, peer)):
        chosen = hrows[:, 0:hslot] + (hrows[:, hslot : 2 * hslot] - hrows[:, 0:hslot]) * core
        for j in range(half // 128):
            row = jnp.concatenate([chosen[k : k + 1, :] for k in range(4 * j, 4 * j + 4)], axis=1)
            chalo[g * half + j * 128 : g * half + (j + 1) * 128, :] = column(row)
    looped(half, lambda r: select(shalo, chalo, r))
    loads[1].wait()
    for load in loads[2:]:
        load.start()
    halo_out[0] = dot(shalo[...], h0[...]).astype(BF)
    pl.semaphore_wait(barrier, 9)
    for k in range(7, -1, -1):
        halo_copy(0, k).start()

    loads[2].wait()
    loads[3].wait()
    bits = hslot.bit_length() - 1
    for j in range(edges // 128):
        sender = esrc[j : j + 1, :]
        far = sender - nodes
        far = ((far >> bits) & 1) * half + (far >> (bits + 1)) * hslot + (far & (hslot - 1))
        csrc[j * 128 : (j + 1) * 128, :] = column(jnp.where(sender < nodes, sender, far + nodes))
        cdst[j * 128 : (j + 1) * 128, :] = column(edst[j : j + 1, :])
    looped(edges, lambda r: (select(ssrc, csrc, r), select(sdst, cdst, r), None)[2])

    def edge_lat_part(layer):
        def go(rows):
            pre[rows, :] = dot(edge[rows, :], ef[layer, 0:512, :])

        unrolled(edges, go)

    def own_part(layer, h):
        def go(rows):
            own[rows, :] = dot(ssrc[rows, 0:nodes], h[...]).astype(BF)
            there = dot(sdst[rows, :], h[...]).astype(BF)
            pre[rows, :] += dot(there, ef[layer, 1024:1536, :])

        unrolled(edges, go)

    def edge_update(layer):
        def go(rows):
            far = dot(ssrc[rows, nodes:], halo_in[layer]).astype(BF)
            hidden = pre[rows, :] + dot(own[rows, :] + far, ef[layer, 512:1024, :])
            hidden = jnp.maximum(hidden, 0.0).astype(BF)
            update = dot(hidden, es[layer])
            edge[rows, :] = (edge[rows, :].astype(F32) + layer_norm(update)).astype(BF)

        unrolled(edges, go)

    def node_lat_part(layer, h):
        def go(rows):
            hn[rows, :] = dot(h[rows, :], nf[layer, 0:512, :])

        unrolled(nodes, go)

    def mlp(layer, start, first, one, other):
        summed = (one.astype(F32) + other.astype(F32)).astype(BF)
        hidden = jnp.maximum(first + dot(summed, nf[layer, 512:1024, :]), 0.0).astype(BF)
        return (start.astype(F32) + layer_norm(dot(hidden, ns[layer]))).astype(BF)

    def sum_edges(layer, c):
        rows = slice(c * ROWS, (c + 1) * ROWS)
        part[layer, rows, :] = dot(tdst[rows, :], edge[...]).astype(BF)
        exchange(layer, c).start()

    def node_update(layer, h, new, c):
        rows = slice(c * ROWS, (c + 1) * ROWS)
        exchange(layer, c).wait_recv()
        new[rows, :] = mlp(layer, h[rows, :], hn[rows, :], part[layer, rows, :], part_in[layer, rows, :])

    def share_halo(layer):
        for c in range(2):
            for k in range(4 * c, 4 * c + 4):
                halo_copy(layer, k).wait_recv()
            halo_share(layer, c).start()

    loads[4].wait()
    loads[5].wait()
    edge_lat_part(0)
    own_part(0, h0)
    loads[6].wait()
    node_lat_part(0, h0)
    hnh[...] = dot(halo_out[0], nf[0, 0:512, :])
    looped(halos, lambda r: incident(thalo, chalo[pl.ds(r, SEL), :], r))
    looped(nodes, lambda r: incident(tdst, sublanes + r, r))
    loads[7].wait()
    index_copy.start()
    share_halo(0)
    index_copy.wait_recv()
    for j in range(requests // 128):
        cprobe[2 * j * 128 : (2 * j + 1) * 128, :] = column(prows_in[j : j + 1, :])
        cprobe[(2 * j + 1) * 128 : (2 * j + 2) * 128, :] = column(prows[j : j + 1, :])
    looped(2 * requests, lambda r: incident(tprobe, cprobe[pl.ds(r, SEL), :], r))
    loads[8].wait()
    loads[9].wait()
    for c in range(2):
        halo_share(0, c).wait_recv()
    edge_update(0)

    halo_theirs[...] = dot(thalo[half:, :], edge[...]).astype(BF)
    halo_exchange.start()
    halo_mine[...] = dot(thalo[0:half, :], edge[...]).astype(BF)
    sum_edges(0, 0)
    halo_exchange.wait_recv()
    halo_out[1] = mlp(0, halo_out[0], hnh[...], halo_mine[...], halo_theirs_in[...])
    for k in range(7, -1, -1):
        halo_copy(1, k).start()
    sum_edges(0, 1)
    for load in loads[10:]:
        load.wait()
    edge_lat_part(1)
    node_update(0, h0, h1, 0)

    def pick_rows(r):
        for side in range(2):
            here = cprobe[pl.ds(2 * r + 256 * side + 128, 128), :]
            for j in range(nodes // 128):
                hit = jnp.where(here == lanes[0:128] + j * 128, 1.0, 0.0).astype(BF)
                sprobe[pl.ds(r + 128 * side, 128), j * 128 : (j + 1) * 128] = hit

    looped(requests, pick_rows)
    node_update(0, h0, h1, 1)

    own_part(1, h1)
    share_halo(1)

    def pick_part(rows):
        picked = dot(sprobe[rows, :], h1[...]).astype(BF)
        pick[rows, :] = picked
        hnp[rows, :] = dot(picked, nf[1, 0:512, :])

    pick_part(slice(4 * qslot, 6 * qslot))
    pick_part(slice(0, 4 * qslot))
    for c in range(2):
        halo_share(1, c).wait_recv()
    edge_update(1)

    def probe_sums(i):
        first, number = PIECES[i]
        both = dot(tprobe[2 * first * qslot : 2 * (first + number) * qslot, :], edge[...]).astype(BF)
        for n in range(number):
            rows = slice((first + n) * qslot, (first + n + 1) * qslot)
            theirs[rows, :] = both[2 * n * qslot : (2 * n + 1) * qslot]
            mine[rows, :] = both[(2 * n + 1) * qslot : (2 * n + 2) * qslot]
        probe_exchange(i).start()

    def probe_rows(i):
        first, number = PIECES[i]
        rows = slice(first * qslot, (first + number) * qslot)
        probe_exchange(i).wait_recv()
        probe_out[rows, :] = mlp(1, pick[rows, :], hnp[rows, :], mine[rows, :], theirs_in[rows, :])
        for k in range(first, first + number):
            relayed = [relay for relay in relays if relay[0] == k]
            for _, sends, _, via, _, i in relayed:
                pl.when(sends)(relay_out(k, via, i).start)
                pl.when(jnp.logical_not(sends))(probe_copy(k).start)
            if not relayed:
                probe_copy(k).start()

    probe_sums(0)
    probe_sums(1)
    probe_sums(2)
    probe_rows(0)
    probe_rows(1)
    probe_sums(3)
    probe_rows(2)
    pick_part(slice(6 * qslot, 8 * qslot))
    probe_sums(4)
    probe_rows(3)
    probe_rows(4)
    pass_on(0)

    sum_edges(1, 0)
    sum_edges(1, 1)
    node_lat_part(1, h1)


    def interp_weights(r):
        here = sublanes + r
        for j in range(probes // 128):
            lane = slice(j * 128, (j + 1) * 128)
            total = jnp.zeros((SEL, 128), F32)
            for s in range(8):
                total = total + jnp.where(here == pslot[s : s + 1, lane], pwgt[s : s + 1, lane], 0.0)
            wint[j * 128 : (j + 1) * 128, pl.ds(r, SEL)] = jnp.transpose(total).astype(BF)

    looped(requests, interp_weights)
    node_update(1, h1, h2, 0)
    node_update(1, h1, h2, 1)

    total = emb[...].astype(F32)
    for c in (1, 3, 0, 2):
        rows = slice(2 * c * qslot, (2 * c + 2) * qslot)
        probe_copy(2 * c).wait_recv()
        probe_copy(2 * c + 1).wait_recv()
        total = total + dot(wint[:, rows], probe_in[rows, :])
    hidden = jnp.maximum(dot(total.astype(BF), d1[...]), 0.0).astype(BF)
    fields[...] = lax.dot_general(d2[...], hidden, (((1,), (1,)), ((), ())), preferred_element_type=F32)

    index_copy.wait_send()
    halo_exchange.wait_send()
    for k in range(8):
        halo_copy(0, k).wait_send()
        halo_copy(1, k).wait_send()
        relayed = [relay for relay in relays if relay[0] == k]
        for _, sends, passes, via, on, i in relayed:
            pl.when(sends)(relay_out(k, via, i).wait_send)
            pl.when(jnp.logical_not(sends))(probe_copy(k).wait_send)
            pl.when(passes)(relay_on(k, on, i).wait_send)
        if not relayed:
            probe_copy(k).wait_send()
    for c in range(2):
        for layer in range(2):
            exchange(layer, c).wait_send()
            halo_share(layer, c).wait_send()
    for i in range(len(PIECES)):
        probe_exchange(i).wait_send()


def handover(surface, fields, surface_out, fields_out, sem):
    part = surface.shape[0] // 4
    moves = [pltpu.make_async_copy(fields, fields_out, sem.at[4])]
    for i in range(4):
        cut = pl.ds(i * part, part)
        moves.append(pltpu.make_async_copy(surface.at[cut, :], surface_out.at[cut, :], sem.at[i]))
    for move in moves:
        move.start()
    for move in moves:
        move.wait()


def body(
    node_lat, edge_lat, edge_src, edge_dst, halo_rows, probe_rows, probe_slot, probe_wgt, probe_embed,
    edge_first, edge_second, node_first, node_second, decode_first, decode_second,
):
    nodes, width = node_lat.shape
    edges, probes = edge_lat.shape[0], probe_embed.shape[0]
    halos, requests = halo_rows.size, probe_rows.size
    layers, fields = edge_first.shape[0], decode_second.shape[0]
    anywhere = pl.BlockSpec(memory_space=pl.ANY)
    vmem = pl.BlockSpec(memory_space=pltpu.VMEM)
    dma = pltpu.SemaphoreType.DMA
    def buf(*shape, dtype=BF):
        return pltpu.VMEM(shape, dtype)

    i32 = jnp.int32
    made = pl.pallas_call(
        kernel,
        out_shape=(pltpu.VMEM((nodes, width), BF), pltpu.VMEM((fields, probes), F32)),
        in_specs=[anywhere] * 15,
        out_specs=(vmem, vmem),
        scratch_shapes=[
            buf(edges // 128, 128, dtype=i32), buf(edges // 128, 128, dtype=i32),
            buf(*halo_rows.shape, dtype=i32), buf(*probe_rows.shape, dtype=i32),
            buf(*probe_slot.shape[::-1], dtype=i32), buf(*probe_wgt.shape[::-1], dtype=F32), buf(*decode_second.shape),
            buf(nodes, width), buf(nodes, width), buf(edges, width), buf(probes, width),
            buf(*edge_first.shape), buf(*edge_second.shape), buf(*node_first.shape), buf(*node_second.shape),
            buf(*decode_first.shape),
            buf(edges, 128, dtype=i32), buf(edges, 128, dtype=i32), buf(halos, 128, dtype=i32),
            buf(2 * requests, 128, dtype=i32), buf(*probe_rows.shape, dtype=i32),
            buf(edges, nodes + halos), buf(edges, nodes), buf(nodes, edges), buf(halos // 2, nodes), buf(halos, edges),
            buf(requests, nodes), buf(2 * requests, edges), buf(probes, requests),
            buf(edges, width), buf(edges, width, dtype=F32), buf(nodes, width, dtype=F32),
            buf(halos // 2, width, dtype=F32), buf(requests, width, dtype=F32),
            buf(layers, nodes, width), buf(layers, nodes, width),
            buf(halos // 2, width), buf(halos // 2, width), buf(halos // 2, width),
            buf(layers, halos // 2, width), buf(layers, halos, width),
            buf(requests, width), buf(requests, width), buf(requests, width), buf(requests, width),
            buf(requests, width), buf(requests, width), buf(2, requests // 8, width),
            dma((19,)), dma((layers, 8)), dma((layers, 8)), dma((layers, 2)), dma((layers, 2)),
            dma((1,)), dma((1,)), dma((5,)), dma((5,)), dma((8,)), dma((8,)), dma((1,)), dma((1,)),
            dma((layers, 2)), dma((layers, 2)), dma((2,)), dma((2,)), dma((2,)),
        ],
        compiler_params=pltpu.CompilerParams(
            collective_id=0, has_side_effects=True, vmem_limit_bytes=60 * 1024 * 1024
        ),
    )(
        node_lat, edge_lat, edge_src.reshape(-1, 128), edge_dst.reshape(-1, 128), halo_rows, probe_rows,
        probe_slot.T, probe_wgt.T, probe_embed,
        edge_first, edge_second, node_first, node_second, decode_first, decode_second,
    )
    made = [pltpu.with_memory_space_constraint(array, pltpu.VMEM) for array in made]
    return pl.pallas_call(
        handover,
        out_shape=(jax.ShapeDtypeStruct((nodes, width), BF), jax.ShapeDtypeStruct((fields, probes), F32)),
        in_specs=[vmem] * 2,
        out_specs=(anywhere, anywhere),
        scratch_shapes=[dma((5,))],
    )(*made)


def solution(mesh):
    both = P(("dom", "feat"), None)
    return jax.shard_map(
        body,
        mesh=mesh,
        in_specs=(
            P("dom", None), both, P(("dom", "feat")), P(("dom", "feat")), P("dom", None),
            both, both, both, both, P(), P(), P(), P(), P(), P(),
        ),
        out_specs=(P("dom", None), P(None, ("dom", "feat"))),
        check_vma=False,
    )
```
